256 devices in a mesh: row: 16 (over z, core), col: 16 (over x, y).
Axes of the slice: x: 4, y: 4, z: 8, core: 2. Of those that a mesh axis runs over, the one named last changes fastest.
Arguments:
- gn_matrix: float32 [16384, 16384], P('row', 'col'), as said below
- slab: float32 [1024, 16384], P('col', 'row'), may hold values from -0.1875 to 0.1875
- panel_index: int32 [1], replicated, may hold values from 0 to 31
Outputs:
- factored: float32 [16384, 16384], P('row', 'col')
The draws below stay inside these ranges and needn't reach their ends.
Inputs may be any that keep to these rules, and one draw needn't show every extreme that they name: gn_matrix is symmetric in parameter order and positive definite.
All inputs are finite; a program needn't handle non-finite values.
Results may differ from the reference program's by a relative error of at most 0.00005.
Values sent between devices are 32-bit elements; how exact they have to be, the bound alone decides.
A program may use at most 128 MiB of HBM per device.

```python
import math
import jax
import jax.numpy as jnp
from jax import lax

W = 16384
NB = 256
R = 1024
N_ROW = 16
N_COL = 16


def draw_gn_matrix(key, part):
    key = jax.random.fold_in(key, 11)
    first, second = jax.random.split(key)
    diagonal = jnp.exp(jax.random.uniform(first, (W,), jnp.float32, 0.0, math.log(8.0)))
    noise = jax.random.uniform(second, (W, W), jnp.float32, -1.0, 1.0) * (0.5 / W)
    whole = noise + noise.T
    spots = jnp.arange(W, dtype=jnp.int32)
    whole = whole.at[spots, spots].add(diagonal)
    shaped = whole.reshape(W // (NB * N_ROW), N_ROW, NB, W // (NB * N_COL), N_COL, NB)
    return shaped.transpose(1, 0, 2, 4, 3, 5).reshape(W, W)


def level_of(stream_key, shape, cuts, low, high):
    level, own = 1.0, jax.random.fold_in(stream_key, 6)
    for position, shards_of in cuts:
        steps = jnp.exp(jax.random.uniform(jax.random.fold_in(own, position), (shards_of,), jnp.float32, low / len(cuts), high / len(cuts)))
        level = level * jnp.repeat(steps, shape[position] // shards_of).reshape([-1 if axis == position else 1 for axis in range(len(shape))])
    return level


def normal_values(own_key, shape, width, reach, cuts=(), kind=jnp.bfloat16):
    values = width * jax.random.normal(own_key, shape, jnp.float32)
    if cuts:
        values = values * level_of(own_key, shape, cuts, -0.22, 0.18)
    return jnp.clip(values, -reach, reach).astype(kind)


def setup_inputs(seed: int = 0) -> dict:
    seeds = jax.random.split(jax.random.key(seed), 4)
    return {
        "gn_matrix": draw_gn_matrix(jax.random.fold_in(seeds[3], 71), 0),
        "slab": normal_values(seeds[1], (R, W), R ** -0.5, 0.1875, ((0, 16), (1, 16)), jnp.float32),
        "panel_index": jax.random.randint(seeds[2], (1,), 0, W // NB // 2).astype(jnp.int32),
    }


def forward_map(parts):
    spots = jnp.arange(W, dtype=jnp.int32)
    local = W // parts
    inner_pos = spots % local
    return (inner_pos // NB * parts + spots // local) * NB + inner_pos % NB

def inverse_map(parts):
    params = jnp.arange(W, dtype=jnp.int32)
    blocks = params // NB
    return blocks % parts * (W // parts) + blocks // parts * NB + params % NB

def contract(left, right):
    return lax.dot_general(left.astype(jnp.float32), right.astype(jnp.float32), (((0,), (0,)), ((), ())), precision=lax.Precision.HIGHEST, preferred_element_type=jnp.float32)

def reference(gn_matrix, slab, panel_index):
    which = panel_index[0]
    row_inverse = inverse_map(N_ROW)
    col_forward = forward_map(N_COL)
    gather_index = row_inverse[col_forward]
    slab_cols = slab[:, gather_index]
    damped = gn_matrix + contract(slab, slab_cols)
    col_start = which % N_COL * (W // N_COL) + which // N_COL * NB
    row_start = which % N_ROW * (W // N_ROW) + which // N_ROW * NB
    column_part = lax.dynamic_slice_in_dim(damped, col_start, NB, 1)
    pivot = lax.dynamic_slice_in_dim(column_part, row_start, NB, 0)
    lower_piv = jnp.linalg.cholesky(pivot)
    solved = jax.scipy.linalg.solve_triangular(lower_piv, column_part.T, lower=True).T
    block_ids = (forward_map(N_ROW) // NB)[:, None]
    below = jnp.where(block_ids > which, solved, jnp.zeros_like(solved))
    below_cols = below[gather_index]
    updated = damped - contract(below.T, below_cols.T)
    stacked = jnp.tile(lower_piv, (W // NB, 1))
    column = jnp.where(block_ids == which, stacked, jnp.where(block_ids > which, solved, column_part))
    return lax.dynamic_update_slice_in_dim(updated, column, col_start, 1)
```

```python
import functools

import jax
import jax.numpy as jnp
from jax import lax
from jax.experimental import pallas as pl
from jax.experimental.pallas import tpu as pltpu
from jax.sharding import PartitionSpec as P

NB = 256
N = 16
MESH = pl.DeviceIdType.MESH
ANY = pl.BlockSpec(memory_space=pl.ANY)
F32 = jnp.float32


def signal(row, col):
    pl.semaphore_signal(
        pltpu.get_barrier_semaphore(),
        inc=1,
        device_id={"row": row, "col": col},
        device_id_type=MESH,
    )


def remote(src, dst, send, recv, row, col):
    return pltpu.make_async_remote_copy(
        src_ref=src,
        dst_ref=dst,
        send_sem=send,
        recv_sem=recv,
        device_id={"row": row, "col": col},
        device_id_type=MESH,
    )


def spread_kernel(m, b, gn, slab, rb, zb, qb, ssem, rsem, lsem):
    r = lax.axis_index("row")
    c = lax.axis_index("col")
    lo = b * NB
    in_row = r == m
    in_col = c == m

    @pl.when(r != c)
    def _():
        signal(c, r)

    @pl.when(jnp.logical_not(in_col))
    def _():
        signal(r, m)

    @pl.when(jnp.logical_not(in_row))
    def _():
        signal(m, c)

    local_slab = pltpu.make_async_copy(slab, rb.at[:, pl.ds(0, 1024)], lsem.at[0])
    local_slab.start()
    count = (
        (r != c).astype(jnp.int32)
        + in_row.astype(jnp.int32) * (N - 1)
        + in_col.astype(jnp.int32) * (N - 1)
    )

    @pl.when(count > 0)
    def _():
        pl.semaphore_wait(pltpu.get_barrier_semaphore(), count)

    def other(i):
        return lax.rem(i + (m + 1), N)

    def piece_qq(k):
        start = pl.multiple_of(lo + k * 16, 16)
        return gn.at[pl.ds(start, 16), pl.ds(lo, NB)]

    def copy_qq(i):
        k = other(i)
        return remote(piece_qq(k), qb.at[pl.ds(64, 16)], ssem.at[0, i], rsem.at[0], m, k)

    def copy_qqf(i):
        k = other(i)
        return remote(
            qb.at[pl.ds(64, 16)], qb.at[pl.ds(64, 16)], ssem.at[1, i], rsem.at[0], k, c
        )

    def copy_jq(i):
        k = other(i)
        return remote(
            slab.at[:, pl.ds(lo, NB)], qb.at[pl.ds(0, 64)], ssem.at[2, i], rsem.at[1], k, c
        )

    def copy_gnc(i):
        k = other(i)
        start = pl.multiple_of(lo + k * 16, 16)
        return remote(
            gn.at[pl.ds(start, 16)], zb.at[pl.ds(64, 16)], ssem.at[3, i], rsem.at[2], k, c
        )

    def copy_gnr(i):
        k = other(i)
        start = pl.multiple_of(k * 64, 64)
        return remote(
            gn.at[pl.ds(start, 64), pl.ds(lo, NB)],
            rb.at[:, pl.ds(1024, NB)],
            ssem.at[4, i],
            rsem.at[3],
            r,
            k,
        )

    trans = remote(slab, zb.at[pl.ds(0, 64)], ssem.at[5, 0], rsem.at[4], c, r)
    own_qq = pltpu.make_async_copy(piece_qq(m), qb.at[pl.ds(64, 16)], lsem.at[1])
    own_jq = pltpu.make_async_copy(slab.at[:, pl.ds(lo, NB)], qb.at[pl.ds(0, 64)], lsem.at[2])
    own_gnc = pltpu.make_async_copy(gn.at[pl.ds(lo + m * 16, 16)], zb.at[pl.ds(64, 16)], lsem.at[3])
    own_gnr = pltpu.make_async_copy(
        gn.at[pl.ds(m * 64, 64), pl.ds(lo, NB)], rb.at[:, pl.ds(1024, NB)], lsem.at[4]
    )
    own_trans = pltpu.make_async_copy(slab, zb.at[pl.ds(0, 64)], lsem.at[5])

    def each(make, act):
        def body(i, carry):
            act(make(i))
            return carry

        lax.fori_loop(0, N - 1, body, 0)

    def start(copy):
        copy.start()

    def wait_send(copy):
        copy.wait_send()

    @pl.when(in_row & in_col)
    def _():
        own_qq.start()
        each(copy_qq, start)

    @pl.when(in_row)
    def _():
        own_jq.start()
        each(copy_jq, start)

    @pl.when(r != c)
    def _():
        trans.start()

    @pl.when(r == c)
    def _():
        own_trans.start()

    @pl.when(in_row)
    def _():
        own_gnc.start()
        each(copy_gnc, start)

    @pl.when(in_col)
    def _():
        own_gnr.start()
        each(copy_gnr, start)

    @pl.when(in_row & in_col)
    def _():
        own_qq.wait()

    @pl.when(jnp.logical_not(in_row & in_col))
    def _():
        copy_qq(0).wait_recv()

    @pl.when(in_row)
    def _():
        each(copy_qqf, start)
        own_jq.wait()
        own_gnc.wait()
        each(copy_jq, wait_send)
        each(copy_gnc, wait_send)

    @pl.when(jnp.logical_not(in_row))
    def _():
        copy_jq(0).wait_recv()
        copy_gnc(0).wait_recv()

    @pl.when(in_col)
    def _():
        own_gnr.wait()
        each(copy_gnr, wait_send)

    @pl.when(jnp.logical_not(in_col))
    def _():
        copy_gnr(0).wait_recv()

    @pl.when(r != c)
    def _():
        trans.wait()

    @pl.when(r == c)
    def _():
        own_trans.wait()

    @pl.when(in_row & in_col)
    def _():
        each(copy_qq, wait_send)

    @pl.when(in_row)
    def _():
        each(copy_qqf, wait_send)

    local_slab.wait()


def spread(m, b, gn, slab):
    return pl.pallas_call(
        functools.partial(spread_kernel, m, b),
        out_shape=(
            jax.ShapeDtypeStruct((64, 1024 + NB), F32),
            jax.ShapeDtypeStruct((80, 1024), F32),
            jax.ShapeDtypeStruct((80, NB), F32),
        ),
        in_specs=[ANY, ANY],
        out_specs=(ANY, ANY, ANY),
        scratch_shapes=[
            pltpu.SemaphoreType.DMA((6, N - 1)),
            pltpu.SemaphoreType.DMA((5,)),
            pltpu.SemaphoreType.DMA((6,)),
        ],
        compiler_params=pltpu.CompilerParams(
            collective_id=1 + b * N + m, has_side_effects=True
        ),
        name="spread",
    )(gn, slab)


class Place:
    def __init__(self):
        self.r = lax.axis_index("row")
        self.c = lax.axis_index("col")
        self.z, self.core = self.r // 2, lax.rem(self.r, 2)
        self.x, self.y = self.c // 4, lax.rem(self.c, 4)

    def col(self, dim, step):
        if dim == 0:
            return lax.rem(self.x + step + 4, 4) * 4 + self.y
        return self.x * 4 + lax.rem(self.y + step + 4, 4)

    def col2(self, dim, first, second):
        dx, dy = (first, second) if dim == 0 else (second, first)
        return lax.rem(self.x + dx + 4, 4) * 4 + lax.rem(self.y + dy + 4, 4)

    def row(self, step):
        return lax.rem(self.z + step + 8, 8) * 2 + self.core


class Ring:
    def __init__(self, place, buf, dim, item, slot, rows, sems):
        start, height = rows
        ssem, rsem, base = sems
        plus, minus = place.col(dim, 1), place.col(dim, -1)
        half = (height // 2 + 7) // 8 * 8
        rest = height - half

        def part(at, first, size):
            return buf.at[at, pl.ds(first, size)]

        def make(n, at, first, size, target):
            ref = part(at, first, size)
            return remote(ref, ref, ssem.at[base + n], rsem.at[base + n], place.r, target)

        self.sp = make(0, slot(0), start, height, plus)
        self.sm = make(1, slot(0), start, height, minus)
        self.fp = make(2, slot(-1), start, half, plus)
        self.fm = make(3, slot(1), start + half, rest, minus)
        self.rp = make(0, slot(-1), start, height, plus)
        self.rm = make(1, slot(1), start, height, minus)
        self.rfp = make(2, slot(2), start, half, plus)
        self.rfm = make(3, slot(2), start + half, rest, minus)

    def begin(self):
        self.sp.start()
        self.sm.start()

    def forward(self):
        self.rp.wait_recv()
        self.fp.start()
        self.rm.wait_recv()
        self.fm.start()

    def finish(self):
        self.rfp.wait_recv()
        self.rfm.wait_recv()

    def drain(self):
        for copy in (self.sp, self.sm, self.fp, self.fm):
            copy.wait_send()


class Plane:
    def __init__(self, place, buf, height, ssem, rsem, base):
        half = height // 2
        self.first, self.second = [], []
        n = base
        for dim in (0, 1):
            rows = (dim * half, half)
            self.first.append(
                Ring(
                    place, buf, dim, 0,
                    functools.partial(place.col2, dim, second=0),
                    rows, (ssem, rsem, n),
                )
            )
            n += 4
            seconds = []
            for item in (0, -1, 1, 2):
                def slot(step, dim=dim, item=item):
                    return place.col2(dim, item, step)

                seconds.append(Ring(place, buf, 1 - dim, item, slot, rows, (ssem, rsem, n)))
                n += 4
            self.second.append(seconds)

    def begin(self):
        for dim in (0, 1):
            self.first[dim].begin()
        for dim in (0, 1):
            self.second[dim][0].begin()

    def forward1(self):
        for dim in (0, 1):
            self.first[dim].forward()
        for dim in (0, 1):
            self.second[dim][1].begin()
            self.second[dim][2].begin()

    def forward2(self):
        for dim in (0, 1):
            self.second[dim][0].forward()
        for dim in (0, 1):
            self.first[dim].finish()
            self.second[dim][3].begin()

    def forward3(self):
        for item in (1, 2):
            for dim in (0, 1):
                self.second[dim][item].forward()

    def forward4(self):
        for dim in (0, 1):
            self.second[dim][3].forward()

    def finish(self):
        for dim in (0, 1):
            for ring in self.second[dim]:
                ring.finish()

    def drain(self):
        for dim in (0, 1):
            self.first[dim].drain()
            for ring in self.second[dim]:
                ring.drain()


class Line:
    def __init__(self, place, buf, height, ssem, rsem, base):
        self.place = place
        half = height // 2
        plus, minus = place.row(1), place.row(-1)
        sibling = place.r + 1 - 2 * place.core

        def make(n, at, first, size, target):
            ref = buf.at[at, pl.ds(first, size)]
            return remote(ref, ref, ssem.at[base + n], rsem.at[base + n], target, place.c)

        self.send, self.recv = [], []
        for s in range(3):
            self.send.append(
                (make(2 * s, place.row(-s), 0, height, plus), make(2 * s + 1, place.row(s), 0, height, minus))
            )
            self.recv.append(
                (
                    make(2 * s, place.row(-s - 1), 0, height, plus),
                    make(2 * s + 1, place.row(s + 1), 0, height, minus),
                )
            )
        self.send.append(
            (make(6, place.row(-3), 0, half, plus), make(7, place.row(3), half, half, minus))
        )
        self.recv.append(
            (make(6, place.row(4), 0, half, plus), make(7, place.row(4), half, half, minus))
        )
        self.over, self.back = [], []
        other = 1 - 2 * place.core
        for i, step in enumerate((0, -1, 1, -2, 2, -3, 3, 4)):
            self.over.append(make(8 + i, place.row(step), 0, height, sibling))
            self.back.append(make(8 + i, place.row(step) + other, 0, height, sibling))

    def begin(self):
        for copy in self.send[0]:
            copy.start()
        self.over[0].start()

    def step(self, s):
        for way in (0, 1):
            self.recv[s - 1][way].wait_recv()
            self.send[s][way].start()
        for way in (0, 1):
            self.over[2 * s - 1 + way].start()

    def finish(self):
        for way in (0, 1):
            self.recv[3][way].wait_recv()
        self.over[7].start()
        for copy in self.back:
            copy.wait_recv()

    def drain(self):
        for pair in self.send:
            for copy in pair:
                copy.wait_send()
        for copy in self.over:
            copy.wait_send()


def gather_kernel(rb, zb, qb, rg, zg, qg, ssem, rsem, lsem):
    place = Place()
    r, c = place.r, place.c
    for dim in (0, 1):
        for step in (1, -1):
            signal(r, place.col(dim, step))
    signal(place.row(1), c)
    signal(place.row(-1), c)
    signal(r + 1 - 2 * place.core, c)
    own_q = pltpu.make_async_copy(qb, qg.at[c], lsem.at[0])
    own_r = pltpu.make_async_copy(rb, rg.at[c], lsem.at[1])
    own_z = pltpu.make_async_copy(zb, zg.at[r], lsem.at[2])
    own_q.start()
    own_z.start()
    own_r.start()
    small = Plane(place, qg, 80, ssem, rsem, 0)
    large = Plane(place, rg, 64, ssem, rsem, 40)
    line = Line(place, zg, 80, ssem, rsem, 80)
    pl.semaphore_wait(pltpu.get_barrier_semaphore(), 7)
    own_q.wait()
    small.begin()
    own_z.wait()
    line.begin()
    small.forward1()
    small.forward2()
    own_r.wait()
    large.begin()
    small.forward3()
    small.forward4()
    line.step(1)
    large.forward1()
    small.finish()
    line.step(2)
    large.forward2()
    large.forward3()
    line.step(3)
    large.forward4()
    line.finish()
    large.finish()
    small.drain()
    large.drain()
    line.drain()


def gather(rb, zb, qb):
    return pl.pallas_call(
        gather_kernel,
        out_shape=(
            jax.ShapeDtypeStruct((N,) + rb.shape, F32),
            jax.ShapeDtypeStruct((N,) + zb.shape, F32),
            jax.ShapeDtypeStruct((N,) + qb.shape, F32),
        ),
        in_specs=[ANY, ANY, ANY],
        out_specs=(ANY, ANY, ANY),
        scratch_shapes=[
            pltpu.SemaphoreType.DMA((96,)),
            pltpu.SemaphoreType.DMA((96,)),
            pltpu.SemaphoreType.DMA((3,)),
        ],
        compiler_params=pltpu.CompilerParams(collective_id=0, has_side_effects=True),
        name="gather",
    )(rb, zb, qb)


def dot_t(left, right):
    return lax.dot_general(
        left,
        right,
        (((0,), (0,)), ((), ())),
        precision=lax.Precision.HIGH,
        preferred_element_type=F32,
    )


def dot(left, right):
    return jnp.dot(left, right, precision=lax.Precision.HIGH, preferred_element_type=F32)


def on_device(gn, slab, panel_index):
    r = lax.axis_index("row")
    c = lax.axis_index("col")
    which = panel_index[0]
    variants = [functools.partial(spread, k % N, k // N) for k in range(2 * N)]
    rb, zb, qb = lax.switch(which, variants, gn, slab)
    rg, zg, qg = gather(rb, zb, qb)
    rg = rg.reshape(1024, 1024 + NB)
    jr, gnr = rg[:, :1024], rg[:, 1024:]
    jc, gnc = zg[:, :64].reshape(1024, 1024), zg[:, 64:].reshape(NB, 1024)
    jq, gnqq = qg[:, :64].reshape(1024, NB), qg[:, 64:].reshape(NB, NB)
    pivot = gnqq + dot_t(jq, jq)
    lower = jnp.linalg.cholesky(pivot)
    inverse = jax.scipy.linalg.solve_triangular(lower, jnp.eye(NB, dtype=F32), lower=True)
    column_part = gnr + dot_t(jr, jq)
    solved_r = dot(column_part, inverse.T)
    solved_c = dot(inverse, gnc + dot_t(jq, jc))
    row_ids = jnp.repeat(jnp.arange(4, dtype=jnp.int32) * N + r, NB)[:, None]
    col_ids = jnp.repeat(jnp.arange(4, dtype=jnp.int32) * N + c, NB)[None, :]
    below_r = jnp.where(row_ids > which, solved_r, 0.0)
    below_c = jnp.where(col_ids > which, solved_c, 0.0)
    updated = gn + dot_t(jr, jc) - dot(below_r, below_c)
    column = jnp.where(
        row_ids == which,
        jnp.tile(lower, (4, 1)),
        jnp.where(row_ids > which, solved_r, column_part),
    )
    return jnp.where(col_ids == which, jnp.tile(column, (1, 4)), updated)


def solution(mesh):
    return jax.shard_map(
        on_device,
        mesh=mesh,
        in_specs=(P("row", "col"), P("col", "row"), P()),
        out_specs=P("row", "col"),
        check_vma=False,
    )
```

```python
import functools

import jax
import jax.numpy as jnp
from jax import lax
from jax.experimental import pallas as pl
from jax.experimental.pallas import tpu as pltpu
from jax.sharding import PartitionSpec as P

NB = 256
N = 16
MESH = pl.DeviceIdType.MESH
ANY = pl.BlockSpec(memory_space=pl.ANY)
F32 = jnp.float32


def signal(row, col):
    pl.semaphore_signal(
        pltpu.get_barrier_semaphore(),
        inc=1,
        device_id={"row": row, "col": col},
        device_id_type=MESH,
    )


def remote(src, dst, send, recv, row, col):
    return pltpu.make_async_remote_copy(
        src_ref=src,
        dst_ref=dst,
        send_sem=send,
        recv_sem=recv,
        device_id={"row": row, "col": col},
        device_id_type=MESH,
    )


def spread_kernel(m, b, gn, slab, gr, gc, qb, ssem, rsem, lsem):
    r = lax.axis_index("row")
    c = lax.axis_index("col")
    lo = b * NB
    in_row = r == m
    in_col = c == m

    @pl.when(jnp.logical_not(in_col))
    def _():
        signal(r, m)

    @pl.when(jnp.logical_not(in_row))
    def _():
        signal(m, c)

    count = (in_row.astype(jnp.int32) + in_col.astype(jnp.int32)) * (N - 1)

    @pl.when(count > 0)
    def _():
        pl.semaphore_wait(pltpu.get_barrier_semaphore(), count)

    def other(i):
        return lax.rem(i + (m + 1), N)

    def piece_qq(k):
        start = pl.multiple_of(lo + k * 16, 16)
        return gn.at[pl.ds(start, 16), pl.ds(lo, NB)]

    def copy_qq(i):
        k = other(i)
        return remote(piece_qq(k), qb.at[pl.ds(64, 16)], ssem.at[0, i], rsem.at[0], m, k)

    def copy_qqf(i):
        k = other(i)
        return remote(
            qb.at[pl.ds(64, 16)], qb.at[pl.ds(64, 16)], ssem.at[1, i], rsem.at[0], k, c
        )

    def copy_jq(i):
        k = other(i)
        return remote(
            slab.at[:, pl.ds(lo, NB)], qb.at[pl.ds(0, 64)], ssem.at[2, i], rsem.at[1], k, c
        )

    def copy_gnc(i):
        k = other(i)
        start = pl.multiple_of(lo + k * 16, 16)
        return remote(gn.at[pl.ds(start, 16)], gc, ssem.at[3, i], rsem.at[2], k, c)

    def copy_gnr(i):
        k = other(i)
        start = pl.multiple_of(k * 64, 64)
        return remote(
            gn.at[pl.ds(start, 64), pl.ds(lo, NB)], gr, ssem.at[4, i], rsem.at[3], r, k
        )

    own_qq = pltpu.make_async_copy(piece_qq(m), qb.at[pl.ds(64, 16)], lsem.at[0])
    own_jq = pltpu.make_async_copy(slab.at[:, pl.ds(lo, NB)], qb.at[pl.ds(0, 64)], lsem.at[1])
    own_gnc = pltpu.make_async_copy(gn.at[pl.ds(lo + m * 16, 16)], gc, lsem.at[2])
    own_gnr = pltpu.make_async_copy(gn.at[pl.ds(m * 64, 64), pl.ds(lo, NB)], gr, lsem.at[3])

    def each(make, act):
        def body(i, carry):
            act(make(i))
            return carry

        lax.fori_loop(0, N - 1, body, 0)

    def start(copy):
        copy.start()

    def wait_send(copy):
        copy.wait_send()

    @pl.when(in_row & in_col)
    def _():
        own_qq.start()
        each(copy_qq, start)

    @pl.when(in_row)
    def _():
        own_jq.start()
        each(copy_jq, start)
        own_gnc.start()
        each(copy_gnc, start)

    @pl.when(in_col)
    def _():
        own_gnr.start()
        each(copy_gnr, start)

    @pl.when(in_row & in_col)
    def _():
        own_qq.wait()

    @pl.when(jnp.logical_not(in_row & in_col))
    def _():
        copy_qq(0).wait_recv()

    @pl.when(in_row)
    def _():
        each(copy_qqf, start)
        own_jq.wait()
        own_gnc.wait()
        each(copy_jq, wait_send)
        each(copy_gnc, wait_send)

    @pl.when(jnp.logical_not(in_row))
    def _():
        copy_jq(0).wait_recv()
        copy_gnc(0).wait_recv()

    @pl.when(in_col)
    def _():
        own_gnr.wait()
        each(copy_gnr, wait_send)

    @pl.when(jnp.logical_not(in_col))
    def _():
        copy_gnr(0).wait_recv()

    @pl.when(in_row & in_col)
    def _():
        each(copy_qq, wait_send)

    @pl.when(in_row)
    def _():
        each(copy_qqf, wait_send)


def spread(m, b, gn, slab):
    return pl.pallas_call(
        functools.partial(spread_kernel, m, b),
        out_shape=(
            jax.ShapeDtypeStruct((64, NB), F32),
            jax.ShapeDtypeStruct((16, 1024), F32),
            jax.ShapeDtypeStruct((80, NB), F32),
        ),
        in_specs=[ANY, ANY],
        out_specs=(ANY, ANY, ANY),
        scratch_shapes=[
            pltpu.SemaphoreType.DMA((5, N - 1)),
            pltpu.SemaphoreType.DMA((4,)),
            pltpu.SemaphoreType.DMA((4,)),
        ],
        compiler_params=pltpu.CompilerParams(
            collective_id=1 + b * N + m, has_side_effects=True
        ),
        name="spread",
    )(gn, slab)


class Place:
    def __init__(self):
        self.r = lax.axis_index("row")
        self.c = lax.axis_index("col")
        self.z, self.core = self.r // 2, lax.rem(self.r, 2)
        self.x, self.y = self.c // 4, lax.rem(self.c, 4)

    def col(self, dim, step):
        if dim == 0:
            return lax.rem(self.x + step + 4, 4) * 4 + self.y
        return self.x * 4 + lax.rem(self.y + step + 4, 4)

    def col2(self, dim, first, second):
        dx, dy = (first, second) if dim == 0 else (second, first)
        return lax.rem(self.x + dx + 4, 4) * 4 + lax.rem(self.y + dy + 4, 4)

    def row(self, step):
        return lax.rem(self.z + step + 8, 8) * 2 + self.core


class Ring:
    def __init__(self, place, buf, dim, item, slot, rows, sems):
        start, height = rows
        ssem, rsem, base = sems
        plus, minus = place.col(dim, 1), place.col(dim, -1)
        half = (height // 2 + 7) // 8 * 8
        rest = height - half

        def part(at, first, size):
            return buf.at[at, pl.ds(first, size)]

        def make(n, at, first, size, target):
            ref = part(at, first, size)
            return remote(ref, ref, ssem.at[base + n], rsem.at[base + n], place.r, target)

        self.sp = make(0, slot(0), start, height, plus)
        self.sm = make(1, slot(0), start, height, minus)
        self.fp = make(2, slot(-1), start, half, plus)
        self.fm = make(3, slot(1), start + half, rest, minus)
        self.rp = make(0, slot(-1), start, height, plus)
        self.rm = make(1, slot(1), start, height, minus)
        self.rfp = make(2, slot(2), start, half, plus)
        self.rfm = make(3, slot(2), start + half, rest, minus)

    def begin(self):
        self.sp.start()
        self.sm.start()

    def forward(self):
        self.rp.wait_recv()
        self.fp.start()
        self.rm.wait_recv()
        self.fm.start()

    def finish(self):
        self.rfp.wait_recv()
        self.rfm.wait_recv()

    def drain(self):
        for copy in (self.sp, self.sm, self.fp, self.fm):
            copy.wait_send()


class Plane:
    def __init__(self, place, buf, height, ssem, rsem, base):
        half = height // 2
        self.first, self.second = [], []
        n = base
        for dim in (0, 1):
            rows = (dim * half, half)
            self.first.append(
                Ring(
                    place, buf, dim, 0,
                    functools.partial(place.col2, dim, second=0),
                    rows, (ssem, rsem, n),
                )
            )
            n += 4
            seconds = []
            for item in (0, -1, 1, 2):
                def slot(step, dim=dim, item=item):
                    return place.col2(dim, item, step)

                seconds.append(Ring(place, buf, 1 - dim, item, slot, rows, (ssem, rsem, n)))
                n += 4
            self.second.append(seconds)

    def begin(self):
        for dim in (0, 1):
            self.first[dim].begin()

    def begin2(self):
        for dim in (0, 1):
            self.second[dim][0].begin()

    def forward1(self):
        for dim in (0, 1):
            self.first[dim].forward()
        for dim in (0, 1):
            self.second[dim][1].begin()
            self.second[dim][2].begin()

    def forward2(self):
        for dim in (0, 1):
            self.second[dim][0].forward()
        for dim in (0, 1):
            self.first[dim].finish()
            self.second[dim][3].begin()

    def forward3(self):
        for item in (1, 2):
            for dim in (0, 1):
                self.second[dim][item].forward()

    def forward4(self):
        for dim in (0, 1):
            self.second[dim][3].forward()

    def finish(self, item):
        for dim in (0, 1):
            self.second[dim][item].finish()

    def drain(self):
        for dim in (0, 1):
            self.first[dim].drain()
            for ring in self.second[dim]:
                ring.drain()


class Line:
    def __init__(self, place, buf, height, ssem, rsem, base):
        self.place = place
        half = height // 2
        plus, minus = place.row(1), place.row(-1)
        sibling = place.r + 1 - 2 * place.core

        def make(n, at, first, size, target):
            ref = buf.at[at, pl.ds(first, size)]
            return remote(ref, ref, ssem.at[base + n], rsem.at[base + n], target, place.c)

        self.send, self.recv = [], []
        for s in range(3):
            self.send.append(
                (make(2 * s, place.row(-s), 0, height, plus), make(2 * s + 1, place.row(s), 0, height, minus))
            )
            self.recv.append(
                (
                    make(2 * s, place.row(-s - 1), 0, height, plus),
                    make(2 * s + 1, place.row(s + 1), 0, height, minus),
                )
            )
        self.send.append(
            (make(6, place.row(-3), 0, half, plus), make(7, place.row(3), half, half, minus))
        )
        self.recv.append(
            (make(6, place.row(4), 0, half, plus), make(7, place.row(4), half, half, minus))
        )
        self.over, self.back = [], []
        other = 1 - 2 * place.core
        for i, step in enumerate((0, -1, 1, -2, 2, -3, 3, 4)):
            self.over.append(make(8 + i, place.row(step), 0, height, sibling))
            self.back.append(make(8 + i, place.row(step) + other, 0, height, sibling))

    def begin(self):
        for copy in self.send[0]:
            copy.start()
        self.over[0].start()

    def step(self, s):
        for way in (0, 1):
            self.recv[s - 1][way].wait_recv()
            self.send[s][way].start()
        for way in (0, 1):
            self.over[2 * s - 1 + way].start()

    def finish(self):
        for way in (0, 1):
            self.recv[3][way].wait_recv()
        self.over[7].start()
        for copy in self.back:
            copy.wait_recv()

    def drain(self):
        for pair in self.send:
            for copy in pair:
                copy.wait_send()
        for copy in self.over:
            copy.wait_send()


def base(block, result):
    lane = lax.broadcasted_iota(jnp.int32, (64, 64), 1)
    sub = lax.broadcasted_iota(jnp.int32, (64, 64), 0)
    whole = jnp.concatenate([block, (lane == sub).astype(F32)], axis=1)
    rows = [whole[8 * i : 8 * i + 8] for i in range(8)]
    sub8 = lax.broadcasted_iota(jnp.int32, (8, 128), 0)

    def lanes(tile, at):
        return jnp.broadcast_to(tile[:, at : at + 1], (8, 128))

    def subs(tile, at):
        return jnp.broadcast_to(tile[at : at + 1, :], (8, 128))

    for j in range(8):
        tile = rows[j]
        cols = [lanes(tile, 8 * j + k) for k in range(8)]
        full, upper, recips = tile, tile, jnp.zeros_like(tile)
        for k in range(8):
            here = sub8 == k
            recip = 1.0 / subs(cols[k], k)
            factor = jnp.where(here, 0.0, cols[k] * recip)
            recips = jnp.where(here, recip, recips)
            upper = jnp.where(here, full, upper)
            for n in range(k + 1, 8):
                cols[n] = cols[n] - factor * subs(cols[n], k)
            full = full - factor * subs(full, k)
        solved = full * recips
        rows[j] = upper * jnp.sqrt(recips)
        spread = [subs(solved, k) for k in range(8)]
        for i in range(j + 1, 8):
            old = rows[i]
            new = old
            for k in range(8):
                new = new - lanes(old, 8 * j + k) * spread[k]
            rows[i] = new
        if j < 7:
            yield
    out = jnp.concatenate(rows, axis=0)
    result.append(jnp.where(lane >= sub, out[:, :64], 0.0))
    result.append(out[:, 64:])
    yield

def exact(left, right, dims):
    return lax.dot_general(
        left,
        right,
        (dims, ((), ())),
        precision=lax.Precision.HIGHEST,
        preferred_element_type=F32,
    )


def factor(work):
    for s in range(4):
        rows = pl.ds(64 * s, 64)
        result = []
        yield from base(work[rows, pl.ds(64 * s, 64)], result)
        upper, inverse = result
        solved = exact(inverse, work[rows, :], ((1,), (0,)))
        work[rows, :] = solved
        work[rows, pl.ds(64 * s, 64)] = upper
        if s < 3:
            rest = pl.ds(64 * (s + 1), 64 * (3 - s))
            work[rest, :] = work[rest, :] - exact(solved[:, 64 * (s + 1) : 256], solved, ((0,), (0,)))
        yield


A_ORDER = (
    (0, 0),
    (1, 0), (-1, 0),
    (0, 1), (0, -1), (2, 0),
    (1, 1), (1, -1), (-1, 1), (-1, -1),
    (2, 1), (2, -1),
    (0, 2), (1, 2), (-1, 2), (2, 2),
)


class Spine:
    def __init__(self, place, rg, jc, zs, zr, ss, sr, ls):
        self.place, self.rg, self.jc = place, rg, jc
        self.zs, self.zr, self.ss, self.sr, self.ls = zs, zr, ss, sr, ls
        self.dist = lax.rem(place.z - place.c // 2 + 8, 8)
        self.spine = place.core == lax.rem(place.c, 2)
        self.source = self.spine & (self.dist == 0)

    def lag(self, way):
        return self.dist if way == 0 else lax.rem(8 - self.dist, 8)

    def slot(self, way, p):
        first, second = 0, 0
        for i, (a, b) in enumerate(A_ORDER):
            if isinstance(p, int):
                if p == i:
                    first, second = a, b
            else:
                first = jnp.where(p == i, a, first)
                second = jnp.where(p == i, b, second)
        return self.place.col2(way, first, second)

    def copies(self, way, p):
        place = self.place
        where = (self.slot(way, p), pl.ds(32 * way, 32))
        mine, here = self.rg.at[where], self.jc.at[where]
        target = place.row(1 if way == 0 else -1)
        sibling = place.r + 1 - 2 * place.core

        def up(src):
            return remote(src, here, self.zs.at[way, p], self.zr.at[way, p], target, place.c)

        def over(src):
            return remote(src, here, self.ss.at[way, p], self.sr.at[way, p], sibling, place.c)

        def keep():
            return pltpu.make_async_copy(mine, here, self.ls.at[way, p])

        return up, over, mine, here, keep

    def tick(self, t):
        for way in (0, 1):
            lag = self.lag(way)
            p = t - lag
            valid = self.spine & (p >= 0) & (p < N)

            @pl.when(valid & (self.dist == 0))
            def _(way=way):
                if t < N:
                    up, over, mine, here, keep = self.copies(way, t)
                    up(mine).start()
                    over(mine).start()
                    keep().start()

            @pl.when(valid & (self.dist != 0))
            def _(way=way, p=p, lag=lag):
                up, over, mine, here, keep = self.copies(way, p)
                up(here).wait_recv()

                @pl.when(lag < 7)
                def _():
                    up(here).start()

                over(here).start()

    def drain(self):
        for way in (0, 1):
            lag = self.lag(way)
            for p in range(N):
                up, over, mine, here, keep = self.copies(way, p)

                @pl.when(jnp.logical_not(self.spine))
                def _(over=over, here=here):
                    over(here).wait_recv()

                @pl.when(self.spine & (lag < 7))
                def _(up=up, here=here):
                    up(here).wait_send()

                @pl.when(self.spine)
                def _(over=over, here=here):
                    over(here).wait_send()

                @pl.when(self.source)
                def _(keep=keep):
                    keep().wait()


def gather_kernel(
    slab, gr, gc, qb, rg, jc, grg, gcg, qg, lower, inverse,
    work, ssem, rsem, zs, zr, ss, sr, ls, lsem,
):
    place = Place()
    r, c = place.r, place.c
    for dim in (0, 1):
        for step in (1, -1):
            signal(r, place.col(dim, step))
    signal(place.row(1), c)
    signal(place.row(-1), c)
    signal(r + 1 - 2 * place.core, c)
    own_q = pltpu.make_async_copy(qb, qg.at[c], lsem.at[0])
    own_j = pltpu.make_async_copy(slab, rg.at[c], lsem.at[1])
    own_r = pltpu.make_async_copy(gr, grg.at[c], lsem.at[2])
    own_c = pltpu.make_async_copy(gc, gcg.at[r], lsem.at[3])
    own_q.start()
    own_j.start()
    own_c.start()
    own_r.start()
    q = Plane(place, qg, 80, ssem, rsem, 0)
    j = Plane(place, rg, 64, ssem, rsem, 40)
    g = Plane(place, grg, 64, ssem, rsem, 80)
    line = Line(place, gcg, 16, ssem, rsem, 120)
    spine = Spine(place, rg, jc, zs, zr, ss, sr, ls)
    sub = lax.broadcasted_iota(jnp.int32, (NB, NB), 0)
    lane = lax.broadcasted_iota(jnp.int32, (NB, NB), 1)
    work[:, pl.ds(NB, NB)] = (sub == lane).astype(F32)
    pl.semaphore_wait(pltpu.get_barrier_semaphore(), 7)
    own_q.wait()
    q.begin()
    own_j.wait()
    j.begin()
    spine.tick(0)
    own_c.wait()
    line.begin()
    q.begin2()
    q.forward1()
    q.forward2()
    j.begin2()
    q.forward3()
    q.forward4()
    line.step(1)
    j.forward1()
    spine.tick(1)
    for item in range(4):
        q.finish(item)
    jq = qg[:, pl.ds(0, 64), :].reshape(1024, NB)
    work[:, pl.ds(0, NB)] = qg[:, pl.ds(64, 16), :].reshape(NB, NB) + exact(jq, jq, ((0,), (0,)))
    chain = factor(work)

    def advance(steps):
        for _ in range(steps):
            next(chain, None)

    spine.tick(2)
    line.step(2)
    advance(2)
    j.forward2()
    spine.tick(3)
    line.step(3)
    advance(2)
    spine.tick(4)
    advance(2)
    spine.tick(5)
    line.finish()
    advance(2)
    j.forward3()
    for t in (6, 7, 8, 9):
        spine.tick(t)
        advance(2)
    j.forward4()
    own_r.wait()
    g.begin()
    g.begin2()
    spine.tick(10)
    advance(2)
    spine.tick(11)
    advance(2)
    j.finish(0)
    spine.tick(12)
    advance(2)
    j.finish(1)
    j.finish(2)
    spine.tick(13)
    g.forward1()
    advance(2)
    spine.tick(14)
    g.forward2()
    advance(2)
    j.finish(3)
    spine.tick(15)
    g.forward3()
    advance(2)
    spine.tick(16)
    g.forward4()
    for t in range(17, 23):
        advance(2)
        spine.tick(t)
    advance(40)
    lower[...] = jnp.where(sub >= lane, work[:, pl.ds(0, NB)].T, 0.0)
    inverse[...] = jnp.where(sub >= lane, work[:, pl.ds(NB, NB)], 0.0)
    for item in range(4):
        g.finish(item)
    q.drain()
    j.drain()
    g.drain()
    line.drain()
    spine.drain()


def gather(slab, gr, gc, qb):
    vmem = pl.BlockSpec(memory_space=pltpu.VMEM)
    dma = pltpu.SemaphoreType.DMA
    return pl.pallas_call(
        gather_kernel,
        out_shape=tuple(
            jax.ShapeDtypeStruct(shape, F32)
            for shape in (
                (N, 64, 1024),
                (N, 64, 1024),
                (N, 64, NB),
                (N, 16, 1024),
                (N, 80, NB),
                (NB, NB),
                (NB, NB),
            )
        ),
        in_specs=[ANY] * 4,
        out_specs=(ANY, ANY, ANY, ANY, vmem, vmem, vmem),
        scratch_shapes=[pltpu.VMEM((NB, 2 * NB), F32), dma((136,)), dma((136,))]
        + [dma((2, N)) for _ in range(5)]
        + [dma((4,))],
        compiler_params=pltpu.CompilerParams(
            collective_id=0, has_side_effects=True, vmem_limit_bytes=32 * 1024 * 1024
        ),
        name="gather",
    )(slab, gr, gc, qb)


def dot_t(left, right):
    return lax.dot_general(
        left,
        right,
        (((0,), (0,)), ((), ())),
        precision=lax.Precision.HIGH,
        preferred_element_type=F32,
    )


def dot(left, right):
    return jnp.dot(left, right, precision=lax.Precision.HIGH, preferred_element_type=F32)


def on_device(gn, slab, panel_index):
    r = lax.axis_index("row")
    c = lax.axis_index("col")
    which = panel_index[0]
    variants = [functools.partial(spread, k % N, k // N) for k in range(2 * N)]
    gr, gc, qb = lax.switch(which, variants, gn, slab)
    rg, jc, grg, gcg, qg, lower, inverse = gather(slab, gr, gc, qb)
    jr, jc = rg.reshape(1024, 1024), jc.reshape(1024, 1024)
    gnr, gnc = grg.reshape(1024, NB), gcg.reshape(NB, 1024)
    jq = qg[:, :64].reshape(1024, NB)
    column_part = gnr + dot_t(jr, jq)
    solved_r = dot(column_part, inverse.T)
    solved_c = dot(inverse, gnc + dot_t(jq, jc))
    row_ids = jnp.repeat(jnp.arange(4, dtype=jnp.int32) * N + r, NB)[:, None]
    col_ids = jnp.repeat(jnp.arange(4, dtype=jnp.int32) * N + c, NB)[None, :]
    below_r = jnp.where(row_ids > which, solved_r, 0.0)
    below_c = jnp.where(col_ids > which, solved_c, 0.0)
    updated = gn + dot_t(jr, jc) - dot(below_r, below_c)
    column = jnp.where(
        row_ids == which,
        jnp.tile(lower, (4, 1)),
        jnp.where(row_ids > which, solved_r, column_part),
    )
    return jnp.where(col_ids == which, jnp.tile(column, (1, 4)), updated)


def solution(mesh):
    return jax.shard_map(
        on_device,
        mesh=mesh,
        in_specs=(P("row", "col"), P("col", "row"), P()),
        out_specs=P("row", "col"),
        check_vma=False,
    )
```

```python
import functools

import jax
import jax.numpy as jnp
from jax import lax
from jax.experimental import pallas as pl
from jax.experimental.pallas import tpu as pltpu
from jax.sharding import PartitionSpec as P

NB = 256
N = 16
MESH = pl.DeviceIdType.MESH
ANY = pl.BlockSpec(memory_space=pl.ANY)
F32 = jnp.float32


def signal(row, col):
    pl.semaphore_signal(
        pltpu.get_barrier_semaphore(),
        inc=1,
        device_id={"row": row, "col": col},
        device_id_type=MESH,
    )


def remote(src, dst, send, recv, row, col):
    return pltpu.make_async_remote_copy(
        src_ref=src,
        dst_ref=dst,
        send_sem=send,
        recv_sem=recv,
        device_id={"row": row, "col": col},
        device_id_type=MESH,
    )


def spread_kernel(m, b, gn, slab, gr, gc, qb, tb, qp, ssem, rsem, lsem):
    r = lax.axis_index("row")
    c = lax.axis_index("col")
    lo = b * NB
    core = m % 2
    in_row = r == m
    in_col = c == m
    to_row = 2 * lax.rem(r // 2 * 2 + c // 2 + 1, 8) + lax.rem(c, 2)
    from_col = 2 * lax.rem(r // 2 - c // 2 * 2 + 15, 8) + lax.rem(r, 2)
    signal(c, from_col)

    @pl.when(jnp.logical_not(in_col))
    def _():
        signal(r, m)

    @pl.when(jnp.logical_not(in_row))
    def _():
        signal(m, c)

    count = (in_row.astype(jnp.int32) + in_col.astype(jnp.int32)) * (N - 1) + 1
    pl.semaphore_wait(pltpu.get_barrier_semaphore(), count)

    def other(i):
        return lax.rem(i + (m + 1), N)

    def piece_qq(k):
        start = pl.multiple_of(lo + k * 16, 16)
        return gn.at[pl.ds(start, 16), pl.ds(lo, NB)]

    def half(k, size):
        return pl.ds(pl.multiple_of(lax.rem(k, 2) * size, size), size)

    def copy_qq(i):
        k = other(i)
        return remote(piece_qq(k), qp, ssem.at[0, i], rsem.at[0], m, k)

    def copy_qqf(i):
        k = other(i)
        return remote(qp.at[half(k, 8)], qb.at[pl.ds(32, 8)], ssem.at[1, i], rsem.at[5], k, c)

    def copy_jq(i):
        k = other(i)
        src = slab.at[half(k, 32), pl.ds(lo, NB)]
        return remote(src, qb.at[pl.ds(0, 32)], ssem.at[2, i], rsem.at[1], k, c)

    def copy_gnc(i):
        k = other(i)
        start = pl.multiple_of(lo + k * 16, 16)
        return remote(gn.at[pl.ds(start, 16)], gc, ssem.at[3, i], rsem.at[2], k, c)

    def copy_gnr(i):
        k = other(i)
        start = pl.multiple_of(k * 64, 64)
        return remote(
            gn.at[pl.ds(start, 64), pl.ds(lo, NB)], gr, ssem.at[4, i], rsem.at[3], r, k
        )

    own_qq = pltpu.make_async_copy(piece_qq(m), qp, lsem.at[0])
    own_qqf = pltpu.make_async_copy(qp.at[pl.ds(8 * core, 8)], qb.at[pl.ds(32, 8)], lsem.at[1])
    own_jq = pltpu.make_async_copy(
        slab.at[pl.ds(32 * core, 32), pl.ds(lo, NB)], qb.at[pl.ds(0, 32)], lsem.at[2]
    )
    own_gnc = pltpu.make_async_copy(gn.at[pl.ds(lo + m * 16, 16)], gc, lsem.at[3])
    own_gnr = pltpu.make_async_copy(gn.at[pl.ds(m * 64, 64), pl.ds(lo, NB)], gr, lsem.at[4])
    trans = remote(slab, tb, ssem.at[5, 0], rsem.at[4], to_row, r)

    def each(act, *makes):
        def body(i, carry):
            for make in makes:
                act(make(i))
            return carry

        lax.fori_loop(0, N - 1, body, 0)

    def start(copy):
        copy.start()

    def wait_send(copy):
        copy.wait_send()

    @pl.when(in_row & in_col)
    def _():
        own_qq.start()
        each(start, copy_qq)

    @pl.when(in_row)
    def _():
        own_jq.start()
        own_gnc.start()
        each(start, copy_jq, copy_gnc)

    @pl.when(in_col)
    def _():
        own_gnr.start()
        each(start, copy_gnr)

    trans.start()

    @pl.when(in_row & in_col)
    def _():
        own_qq.wait()

    @pl.when(in_row & jnp.logical_not(in_col))
    def _():
        copy_qq(0).wait_recv()

    @pl.when(in_row)
    def _():
        own_qqf.start()
        each(start, copy_qqf)
        own_qqf.wait()
        own_jq.wait()
        own_gnc.wait()
        each(wait_send, copy_jq, copy_gnc, copy_qqf)

    @pl.when(jnp.logical_not(in_row))
    def _():
        copy_jq(0).wait_recv()
        copy_gnc(0).wait_recv()
        copy_qqf(0).wait_recv()

    @pl.when(in_col)
    def _():
        own_gnr.wait()
        each(wait_send, copy_gnr)

    @pl.when(jnp.logical_not(in_col))
    def _():
        copy_gnr(0).wait_recv()

    @pl.when(in_row & in_col)
    def _():
        each(wait_send, copy_qq)

    trans.wait()


def spread(m, b, gn, slab):
    return pl.pallas_call(
        functools.partial(spread_kernel, m, b),
        out_shape=(
            jax.ShapeDtypeStruct((64, NB), F32),
            jax.ShapeDtypeStruct((16, 1024), F32),
            jax.ShapeDtypeStruct((40, NB), F32),
            jax.ShapeDtypeStruct((64, 1024), F32),
        ),
        in_specs=[ANY, ANY],
        out_specs=(ANY, ANY, ANY, ANY),
        scratch_shapes=[
            pltpu.VMEM((16, NB), F32),
            pltpu.SemaphoreType.DMA((6, N - 1)),
            pltpu.SemaphoreType.DMA((6,)),
            pltpu.SemaphoreType.DMA((5,)),
        ],
        compiler_params=pltpu.CompilerParams(
            collective_id=1 + b * N + m, has_side_effects=True
        ),
        name="spread",
    )(gn, slab)


class Place:
    def __init__(self):
        self.r = lax.axis_index("row")
        self.c = lax.axis_index("col")
        self.z, self.core = self.r // 2, lax.rem(self.r, 2)
        self.x, self.y = self.c // 4, lax.rem(self.c, 4)

    def col(self, dim, step):
        if dim == 0:
            return lax.rem(self.x + step + 4, 4) * 4 + self.y
        return self.x * 4 + lax.rem(self.y + step + 4, 4)

    def col2(self, dim, first, second):
        dx, dy = (first, second) if dim == 0 else (second, first)
        return lax.rem(self.x + dx + 4, 4) * 4 + lax.rem(self.y + dy + 4, 4)

    def row(self, step):
        return lax.rem(self.z + step + 8, 8) * 2 + self.core


class Ring:
    def __init__(self, place, buf, dim, item, slot, rows, sems):
        start, height = rows
        ssem, rsem, base = sems
        plus, minus = place.col(dim, 1), place.col(dim, -1)
        half = (height // 2 + 7) // 8 * 8
        rest = height - half

        def part(at, first, size):
            return buf.at[at, pl.ds(first, size)]

        def make(n, at, first, size, target):
            ref = part(at, first, size)
            return remote(ref, ref, ssem.at[base + n], rsem.at[base + n], place.r, target)

        self.sp = make(0, slot(0), start, height, plus)
        self.sm = make(1, slot(0), start, height, minus)
        self.fp = make(2, slot(-1), start, half, plus)
        self.fm = make(3, slot(1), start + half, rest, minus)
        self.rp = make(0, slot(-1), start, height, plus)
        self.rm = make(1, slot(1), start, height, minus)
        self.rfp = make(2, slot(2), start, half, plus)
        self.rfm = make(3, slot(2), start + half, rest, minus)

    def begin(self):
        self.sp.start()
        self.sm.start()

    def forward(self):
        self.rp.wait_recv()
        self.fp.start()
        self.rm.wait_recv()
        self.fm.start()

    def finish(self):
        self.rfp.wait_recv()
        self.rfm.wait_recv()

    def drain(self):
        for copy in (self.sp, self.sm, self.fp, self.fm):
            copy.wait_send()


class Plane:
    def __init__(self, place, buf, height, ssem, rsem, base):
        half = (height // 2 + 7) // 8 * 8
        self.first, self.second = [], []
        n = base
        for dim in (0, 1):
            rows = (dim * half, half if dim == 0 else height - half)
            self.first.append(
                Ring(
                    place, buf, dim, 0,
                    functools.partial(place.col2, dim, second=0),
                    rows, (ssem, rsem, n),
                )
            )
            n += 4
            seconds = []
            for item in (0, -1, 1, 2):
                def slot(step, dim=dim, item=item):
                    return place.col2(dim, item, step)

                seconds.append(Ring(place, buf, 1 - dim, item, slot, rows, (ssem, rsem, n)))
                n += 4
            self.second.append(seconds)

    def begin(self):
        for dim in (0, 1):
            self.first[dim].begin()

    def begin2(self):
        for dim in (0, 1):
            self.second[dim][0].begin()

    def forward1(self):
        for dim in (0, 1):
            self.first[dim].forward()
        for dim in (0, 1):
            self.second[dim][1].begin()
            self.second[dim][2].begin()

    def forward2(self):
        for dim in (0, 1):
            self.second[dim][0].forward()
        for dim in (0, 1):
            self.first[dim].finish()
            self.second[dim][3].begin()

    def forward3(self):
        for item in (1, 2):
            for dim in (0, 1):
                self.second[dim][item].forward()

    def forward4(self):
        for dim in (0, 1):
            self.second[dim][3].forward()

    def finish(self, item):
        for dim in (0, 1):
            self.second[dim][item].finish()

    def drain(self):
        for dim in (0, 1):
            self.first[dim].drain()
            for ring in self.second[dim]:
                ring.drain()


class Line:
    def __init__(self, place, buf, turn, rows, ssem, rsem, base):
        start, height = rows
        half = height // 2
        plus, minus = place.row(1), place.row(-1)
        sibling = place.r + 1 - 2 * place.core

        def slot(step):
            return 2 * lax.rem(place.z - turn + step + 32, 8) + place.core

        def make(n, at, first, size, target):
            ref = buf.at[at, pl.ds(start + first, size)]
            return remote(ref, ref, ssem.at[base + n], rsem.at[base + n], target, place.c)

        self.send, self.recv = [], []
        for s in range(3):
            self.send.append(
                (make(2 * s, slot(-s), 0, height, plus), make(2 * s + 1, slot(s), 0, height, minus))
            )
            self.recv.append(
                (
                    make(2 * s, slot(-s - 1), 0, height, plus),
                    make(2 * s + 1, slot(s + 1), 0, height, minus),
                )
            )
        self.send.append((make(6, slot(-3), 0, half, plus), make(7, slot(3), half, half, minus)))
        self.recv.append((make(6, slot(4), 0, half, plus), make(7, slot(4), half, half, minus)))
        self.over, self.back = [], []
        other = 1 - 2 * place.core
        for i, step in enumerate((0, -1, 1, -2, 2, -3, 3)):
            self.over.append(make(8 + i, slot(step), 0, height, sibling))
            self.back.append(make(8 + i, slot(step) + other, 0, height, sibling))
        for i in (0, 1):
            self.over.append(make(15 + i, slot(4), half * i, half, sibling))
            self.back.append(make(15 + i, slot(4) + other, half * i, half, sibling))

    def begin(self):
        for copy in self.send[0]:
            copy.start()
        self.over[0].start()

    def step(self, s):
        for way in (0, 1):
            self.recv[s - 1][way].wait_recv()
            self.send[s][way].start()
            self.over[2 * s - 1 + way].start()

    def last(self):
        for way in (0, 1):
            self.recv[3][way].wait_recv()
            self.over[7 + way].start()

    def finish(self):
        for copy in self.back:
            copy.wait_recv()

    def drain(self):
        for pair in self.send:
            for copy in pair:
                copy.wait_send()
        for copy in self.over:
            copy.wait_send()


def base(block, result):
    lane = lax.broadcasted_iota(jnp.int32, (64, 64), 1)
    sub = lax.broadcasted_iota(jnp.int32, (64, 64), 0)
    whole = jnp.concatenate([block, (lane == sub).astype(F32)], axis=1)
    rows = [whole[8 * i : 8 * i + 8] for i in range(8)]
    sub8 = lax.broadcasted_iota(jnp.int32, (8, 128), 0)

    def lanes(tile, at):
        return jnp.broadcast_to(tile[:, at : at + 1], (8, 128))

    def subs(tile, at):
        return jnp.broadcast_to(tile[at : at + 1, :], (8, 128))

    for j in range(8):
        tile = rows[j]
        cols = [lanes(tile, 8 * j + k) for k in range(8)]
        full, upper, recips = tile, tile, jnp.zeros_like(tile)
        for k in range(8):
            here = sub8 == k
            recip = 1.0 / subs(cols[k], k)
            factor = jnp.where(here, 0.0, cols[k] * recip)
            recips = jnp.where(here, recip, recips)
            upper = jnp.where(here, full, upper)
            for n in range(k + 1, 8):
                cols[n] = cols[n] - factor * subs(cols[n], k)
            full = full - factor * subs(full, k)
        solved = full * recips
        rows[j] = upper * jnp.sqrt(recips)
        spread = [subs(solved, k) for k in range(8)]
        for i in range(j + 1, 8):
            old = rows[i]
            new = old
            for k in range(8):
                new = new - lanes(old, 8 * j + k) * spread[k]
            rows[i] = new
        if j < 7:
            yield
    out = jnp.concatenate(rows, axis=0)
    result.append(jnp.where(lane >= sub, out[:, :64], 0.0))
    result.append(out[:, 64:])
    yield

def exact(left, right, dims):
    return lax.dot_general(
        left,
        right,
        (dims, ((), ())),
        precision=lax.Precision.HIGHEST,
        preferred_element_type=F32,
    )


def factor(work):
    for s in range(4):
        rows = pl.ds(64 * s, 64)
        result = []
        yield from base(work[rows, pl.ds(64 * s, 64)], result)
        upper, inverse = result
        solved = exact(inverse, work[rows, :], ((1,), (0,)))
        work[rows, :] = solved
        work[rows, pl.ds(64 * s, 64)] = upper
        if s < 3:
            rest = pl.ds(64 * (s + 1), 64 * (3 - s))
            work[rest, :] = work[rest, :] - exact(solved[:, 64 * (s + 1) : 256], solved, ((0,), (0,)))
        yield


def gather_kernel(
    slab, gr, gc, qb, tb, rg, jc, grg, gcg, jq, lower, inverse, qg, work, ssem, rsem, lsem
):
    place = Place()
    r, c, core = place.r, place.c, place.core
    turn = lax.rem(c // 2 * 2 + 1, 8)
    sibling = r + 1 - 2 * core
    for dim in (0, 1):
        for step in (1, -1):
            signal(r, place.col(dim, step))
    signal(place.row(1), c)
    signal(place.row(-1), c)
    signal(sibling, c)
    own_q = pltpu.make_async_copy(qb, qg.at[core, c], lsem.at[0])
    own_j = pltpu.make_async_copy(slab, rg.at[c], lsem.at[1])
    own_t = pltpu.make_async_copy(
        tb, jc.at[2 * lax.rem(place.z - turn + 8, 8) + core], lsem.at[2]
    )
    own_r = pltpu.make_async_copy(gr, grg.at[c], lsem.at[3])
    own_c = pltpu.make_async_copy(gc, gcg.at[r], lsem.at[4])
    own_q.start()
    own_j.start()
    own_t.start()
    own_c.start()
    own_r.start()
    q = Plane(place, qg.at[core], 40, ssem, rsem, 0)
    j = Plane(place, rg, 64, ssem, rsem, 40)
    g = Plane(place, grg, 64, ssem, rsem, 80)
    line = Line(place, gcg, 0, (0, 16), ssem, rsem, 120)
    t0 = Line(place, jc, turn, (0, 32), ssem, rsem, 137)
    t1 = Line(place, jc, turn, (32, 32), ssem, rsem, 154)
    swap = remote(qg.at[core], qg.at[core], ssem.at[171], rsem.at[171], sibling, c)
    swapped = remote(qg.at[1 - core], qg.at[1 - core], ssem.at[171], rsem.at[171], sibling, c)
    sub = lax.broadcasted_iota(jnp.int32, (NB, NB), 0)
    lane = lax.broadcasted_iota(jnp.int32, (NB, NB), 1)
    work[:, pl.ds(NB, NB)] = (sub == lane).astype(F32)
    pl.semaphore_wait(pltpu.get_barrier_semaphore(), 7)
    own_q.wait()
    q.begin()
    own_j.wait()
    j.begin()
    own_t.wait()
    t0.begin()
    t1.begin()
    q.begin2()
    q.forward1()
    j.begin2()
    q.forward2()
    j.forward1()
    q.forward3()
    t0.step(1)
    q.forward4()
    t1.step(1)
    j.forward2()
    for item in range(4):
        q.finish(item)
    swap.start()
    t0.step(2)
    own_r.wait()
    g.begin()
    g.begin2()
    swapped.wait_recv()
    jq[...] = jnp.stack([qg[0, :, pl.ds(0, 32), :], qg[1, :, pl.ds(0, 32), :]], axis=1)
    pivot = jnp.stack([qg[0, :, pl.ds(32, 8), :], qg[1, :, pl.ds(32, 8), :]], axis=1)
    whole = jq[...].reshape(1024, NB)
    work[:, pl.ds(0, NB)] = pivot.reshape(NB, NB) + exact(whole, whole, ((0,), (0,)))
    chain = factor(work)

    def advance(steps):
        for _ in range(steps):
            next(chain, None)

    t1.step(2)
    j.forward3()
    advance(2)
    own_c.wait()
    line.begin()
    advance(2)
    t0.step(3)
    advance(2)
    j.forward4()
    g.forward1()
    advance(2)
    t1.step(3)
    line.step(1)
    advance(4)
    g.forward2()
    advance(2)
    t0.last()
    line.step(2)
    advance(4)
    g.forward3()
    advance(2)
    t1.last()
    line.step(3)
    advance(2)
    g.forward4()
    line.last()
    advance(40)
    lower[...] = jnp.where(sub >= lane, work[:, pl.ds(0, NB)].T, 0.0)
    inverse[...] = jnp.where(sub >= lane, work[:, pl.ds(NB, NB)], 0.0)
    t0.finish()
    t1.finish()
    line.finish()
    for item in range(4):
        j.finish(item)
        g.finish(item)
    for part in (q, j, g, line, t0, t1):
        part.drain()
    swap.wait_send()


def gather(slab, gr, gc, qb, tb):
    vmem = pl.BlockSpec(memory_space=pltpu.VMEM)
    dma = pltpu.SemaphoreType.DMA
    return pl.pallas_call(
        gather_kernel,
        out_shape=tuple(
            jax.ShapeDtypeStruct(shape, F32)
            for shape in (
                (N, 64, 1024),
                (N, 64, 1024),
                (N, 64, NB),
                (N, 16, 1024),
                (N, 2, 32, NB),
                (NB, NB),
                (NB, NB),
            )
        ),
        in_specs=[ANY] * 5,
        out_specs=(ANY, ANY, ANY, ANY, vmem, vmem, vmem),
        scratch_shapes=[
            pltpu.VMEM((2, N, 40, NB), F32),
            pltpu.VMEM((NB, 2 * NB), F32),
            dma((172,)),
            dma((172,)),
            dma((5,)),
        ],
        compiler_params=pltpu.CompilerParams(
            collective_id=0, has_side_effects=True, vmem_limit_bytes=32 * 1024 * 1024
        ),
        name="gather",
    )(slab, gr, gc, qb, tb)


def split(value):
    high = value.astype(jnp.bfloat16)
    return high, (value - high.astype(F32)).astype(jnp.bfloat16)


def triple(left, right, dims):
    total = None
    for a, b in ((left[0], right[1]), (left[1], right[0]), (left[0], right[0])):
        part = lax.dot_general(a, b, (dims, ((), ())), preferred_element_type=F32)
        total = part if total is None else total + part
    return total


TT = ((0,), (0,))
NN = ((1,), (0,))
NT = ((1,), (1,))


def update_kernel(
    where, gn, jr, jc, gnr, gnc, jq, lower, inverse, out,
    jc_high, jc_low, jq_high, jq_low, bc_high, bc_low,
):
    which, r, c = where[0], where[1], where[2]
    step = pl.program_id(0)
    inv = split(inverse[...])

    @pl.when(step == 0)
    def _():
        jc_high[...], jc_low[...] = split(jc[...])
        jq_high[...], jq_low[...] = split(jq[...])
        part = gnc[...] + triple(
            (jq_high[...], jq_low[...]), (jc_high[...], jc_low[...]), TT
        )
        solved = triple(inv, split(part), NN)
        ids = lax.broadcasted_iota(jnp.int32, (NB, 1024), 1) // NB * N + c
        bc_high[...], bc_low[...] = split(jnp.where(ids > which, solved, 0.0))

    rows = split(jr[...])
    part = gnr[...] + triple(rows, (jq_high[...], jq_low[...]), TT)
    solved = triple(split(part), inv, NT)
    row = step * N + r
    below = split(jnp.where(row > which, solved, 0.0))
    whole = gn[...] + triple(rows, (jc_high[...], jc_low[...]), TT)
    whole = whole - triple(below, (bc_high[...], bc_low[...]), NN)
    column = jnp.where(row == which, lower[...], jnp.where(row > which, solved, part))
    for block in range(4):
        cols = slice(NB * block, NB * block + NB)
        out[:, cols] = jnp.where(block * N + c == which, column, whole[:, cols])


def update(where, gn, jr, jc, gnr, gnc, jq, lower, inverse):
    def whole(rows, cols):
        return pl.BlockSpec((rows, cols), lambda i, where: (0, 0))

    bf16 = jnp.bfloat16
    return pl.pallas_call(
        update_kernel,
        out_shape=jax.ShapeDtypeStruct((1024, 1024), F32),
        grid_spec=pltpu.PrefetchScalarGridSpec(
            num_scalar_prefetch=1,
            grid=(4,),
            in_specs=[
                pl.BlockSpec((NB, 1024), lambda i, where: (i, 0)),
                pl.BlockSpec((1024, NB), lambda i, where: (0, i)),
                whole(1024, 1024),
                pl.BlockSpec((NB, NB), lambda i, where: (i, 0)),
                whole(NB, 1024),
                whole(1024, NB),
                whole(NB, NB),
                whole(NB, NB),
            ],
            out_specs=pl.BlockSpec((NB, 1024), lambda i, where: (i, 0)),
            scratch_shapes=[
                pltpu.VMEM((1024, 1024), bf16),
                pltpu.VMEM((1024, 1024), bf16),
                pltpu.VMEM((1024, NB), bf16),
                pltpu.VMEM((1024, NB), bf16),
                pltpu.VMEM((NB, 1024), bf16),
                pltpu.VMEM((NB, 1024), bf16),
            ],
        ),
        compiler_params=pltpu.CompilerParams(
            dimension_semantics=("arbitrary",), vmem_limit_bytes=48 * 1024 * 1024
        ),
        name="update",
    )(where, gn, jr, jc, gnr, gnc, jq, lower, inverse)


def on_device(gn, slab, panel_index):
    r = lax.axis_index("row").astype(jnp.int32)
    c = lax.axis_index("col").astype(jnp.int32)
    which = panel_index[0]
    variants = [functools.partial(spread, k % N, k // N) for k in range(2 * N)]
    gr, gc, qb, tb = lax.switch(which, variants, gn, slab)
    rg, jc, grg, gcg, jq, lower, inverse = gather(slab, gr, gc, qb, tb)
    return update(
        jnp.stack([which, r, c]),
        gn,
        rg.reshape(1024, 1024),
        jc.reshape(1024, 1024),
        grg.reshape(1024, NB),
        gcg.reshape(NB, 1024),
        jq.reshape(1024, NB),
        lower,
        inverse,
    )


def solution(mesh):
    return jax.shard_map(
        on_device,
        mesh=mesh,
        in_specs=(P("row", "col"), P("col", "row"), P()),
        out_specs=P("row", "col"),
        check_vma=False,
    )
```

```python
import functools

import jax
import jax.numpy as jnp
from jax import lax
from jax.experimental import pallas as pl
from jax.experimental.pallas import tpu as pltpu
from jax.sharding import PartitionSpec as P

NB = 256
ROWS = 512
N = 16
MESH = pl.DeviceIdType.MESH
ANY = pl.BlockSpec(memory_space=pl.ANY)
F32 = jnp.float32


def signal(row, col):
    pl.semaphore_signal(
        pltpu.get_barrier_semaphore(),
        inc=1,
        device_id={"row": row, "col": col},
        device_id_type=MESH,
    )


def remote(src, dst, send, recv, row, col):
    return pltpu.make_async_remote_copy(
        src_ref=src,
        dst_ref=dst,
        send_sem=send,
        recv_sem=recv,
        device_id={"row": row, "col": col},
        device_id_type=MESH,
    )


class Place:
    def __init__(self):
        self.r = lax.axis_index("row")
        self.c = lax.axis_index("col")
        self.z, self.core = self.r // 2, lax.rem(self.r, 2)
        self.x, self.y = self.c // 4, lax.rem(self.c, 4)

    def col(self, dim, step):
        if dim == 0:
            return lax.rem(self.x + step + 4, 4) * 4 + self.y
        return self.x * 4 + lax.rem(self.y + step + 4, 4)

    def col2(self, dim, first, second):
        dx, dy = (first, second) if dim == 0 else (second, first)
        return lax.rem(self.x + dx + 4, 4) * 4 + lax.rem(self.y + dy + 4, 4)

    def row(self, step):
        return lax.rem(self.z + step + 8, 8) * 2 + self.core


class Ring:
    def __init__(self, place, buf, dim, item, slot, rows, sems):
        start, height = rows
        ssem, rsem, base = sems
        plus, minus = place.col(dim, 1), place.col(dim, -1)
        half = (height // 2 + 7) // 8 * 8
        rest = height - half

        def part(at, first, size):
            return buf.at[at, pl.ds(first, size)]

        def make(n, at, first, size, target):
            ref = part(at, first, size)
            return remote(ref, ref, ssem.at[base + n], rsem.at[base + n], place.r, target)

        self.sp = make(0, slot(0), start, height, plus)
        self.sm = make(1, slot(0), start, height, minus)
        self.fp = make(2, slot(-1), start, half, plus)
        self.fm = make(3, slot(1), start + half, rest, minus)
        self.rp = make(0, slot(-1), start, height, plus)
        self.rm = make(1, slot(1), start, height, minus)
        self.rfp = make(2, slot(2), start, half, plus)
        self.rfm = make(3, slot(2), start + half, rest, minus)

    def begin(self):
        self.sp.start()
        self.sm.start()

    def forward(self):
        self.rp.wait_recv()
        self.fp.start()
        self.rm.wait_recv()
        self.fm.start()

    def finish(self):
        self.rfp.wait_recv()
        self.rfm.wait_recv()

    def drain(self):
        for copy in (self.sp, self.sm, self.fp, self.fm):
            copy.wait_send()


class Plane:
    def __init__(self, place, buf, height, ssem, rsem, base):
        half = (height // 2 + 7) // 8 * 8
        self.first, self.second = [], []
        n = base
        for dim in (0, 1):
            rows = (dim * half, half if dim == 0 else height - half)
            self.first.append(
                Ring(
                    place, buf, dim, 0,
                    functools.partial(place.col2, dim, second=0),
                    rows, (ssem, rsem, n),
                )
            )
            n += 4
            seconds = []
            for item in (0, -1, 1, 2):
                def slot(step, dim=dim, item=item):
                    return place.col2(dim, item, step)

                seconds.append(Ring(place, buf, 1 - dim, item, slot, rows, (ssem, rsem, n)))
                n += 4
            self.second.append(seconds)

    def begin(self):
        for dim in (0, 1):
            self.first[dim].begin()

    def begin2(self):
        for dim in (0, 1):
            self.second[dim][0].begin()

    def forward1(self):
        for dim in (0, 1):
            self.first[dim].forward()
        for dim in (0, 1):
            self.second[dim][1].begin()
            self.second[dim][2].begin()

    def forward2(self):
        for dim in (0, 1):
            self.second[dim][0].forward()
        for dim in (0, 1):
            self.first[dim].finish()
            self.second[dim][3].begin()

    def forward3(self):
        for item in (1, 2):
            for dim in (0, 1):
                self.second[dim][item].forward()

    def forward4(self):
        for dim in (0, 1):
            self.second[dim][3].forward()

    def finish(self, item):
        for dim in (0, 1):
            self.second[dim][item].finish()

    def drain(self):
        for dim in (0, 1):
            self.first[dim].drain()
            for ring in self.second[dim]:
                ring.drain()


class Line:
    def __init__(self, place, buf, turn, rows, ssem, rsem, base):
        start, height = rows
        half = height // 2
        plus, minus = place.row(1), place.row(-1)
        sibling = place.r + 1 - 2 * place.core

        def slot(step):
            return 2 * lax.rem(place.z - turn + step + 32, 8) + place.core

        def make(n, at, first, size, target):
            ref = buf.at[at, pl.ds(start + first, size)]
            return remote(ref, ref, ssem.at[base + n], rsem.at[base + n], target, place.c)

        self.send, self.recv = [], []
        for s in range(3):
            self.send.append(
                (make(2 * s, slot(-s), 0, height, plus), make(2 * s + 1, slot(s), 0, height, minus))
            )
            self.recv.append(
                (
                    make(2 * s, slot(-s - 1), 0, height, plus),
                    make(2 * s + 1, slot(s + 1), 0, height, minus),
                )
            )
        self.send.append((make(6, slot(-3), 0, half, plus), make(7, slot(3), half, half, minus)))
        self.recv.append((make(6, slot(4), 0, half, plus), make(7, slot(4), half, half, minus)))
        self.over, self.back = [], []
        other = 1 - 2 * place.core
        for i, step in enumerate((0, -1, 1, -2, 2, -3, 3)):
            self.over.append(make(8 + i, slot(step), 0, height, sibling))
            self.back.append(make(8 + i, slot(step) + other, 0, height, sibling))
        for i in (0, 1):
            self.over.append(make(15 + i, slot(4), half * i, half, sibling))
            self.back.append(make(15 + i, slot(4) + other, half * i, half, sibling))

    def begin(self):
        for copy in self.send[0]:
            copy.start()
        self.over[0].start()

    def step(self, s):
        for way in (0, 1):
            self.recv[s - 1][way].wait_recv()
            self.send[s][way].start()
            self.over[2 * s - 1 + way].start()

    def last(self):
        for way in (0, 1):
            self.recv[3][way].wait_recv()
            self.over[7 + way].start()

    def finish(self):
        for copy in self.back:
            copy.wait_recv()

    def drain(self):
        for pair in self.send:
            for copy in pair:
                copy.wait_send()
        for copy in self.over:
            copy.wait_send()


def spread_kernel(m, b, gn, slab, gr, gc, qb, tb, ja, qp, ssem, rsem, lsem, psend, precv):
    r = lax.axis_index("row")
    c = lax.axis_index("col")
    lo = b * NB
    core = m % 2
    in_row = r == m
    in_col = c == m
    to_row = 2 * lax.rem(c // 2 - r // 2 + 8, 8) + lax.rem(c, 2)
    from_col = 2 * lax.rem(r // 2 + c // 2, 8) + lax.rem(r, 2)
    stays = (to_row == r) & (c == r)
    place = Place()
    rings, own_j = [], []
    for dim, at in ((0, place.x), (1, place.y)):
        def slot(step, at=at):
            return lax.rem(at + step + 4, 4)

        rows = pl.ds(32 * dim, 32)
        own_j.append(pltpu.make_async_copy(slab.at[rows], ja.at[dim, at], lsem.at[5 + dim]))
        own_j[dim].start()
        rings.append(Ring(place, ja.at[dim], dim, 0, slot, (0, 32), (psend, precv, 4 * dim)))
        for step in (1, -1):
            signal(r, place.col(dim, step))

    @pl.when(jnp.logical_not(stays))
    def _():
        signal(c, from_col)

    @pl.when(jnp.logical_not(in_col))
    def _():
        signal(r, m)

    @pl.when(jnp.logical_not(in_row))
    def _():
        signal(m, c)

    count = (in_row.astype(jnp.int32) + in_col.astype(jnp.int32)) * (N - 1) + 4
    count = count + jnp.logical_not(stays).astype(jnp.int32)
    pl.semaphore_wait(pltpu.get_barrier_semaphore(), count)

    def other(i):
        return lax.rem(i + (m + 1), N)

    def piece_qq(k):
        start = pl.multiple_of(lo + k * 16, 16)
        return gn.at[pl.ds(start, 16), pl.ds(lo, NB)]

    def half(k, size):
        return pl.ds(pl.multiple_of(lax.rem(k, 2) * size, size), size)

    def copy_qq(i):
        k = other(i)
        return remote(piece_qq(k), qp, ssem.at[0, i], rsem.at[0], m, k)

    def copy_qqf(i):
        k = other(i)
        return remote(qp.at[half(k, 8)], qb.at[pl.ds(32, 8)], ssem.at[1, i], rsem.at[5], k, c)

    def copy_jq(i):
        k = other(i)
        src = slab.at[half(k, 32), pl.ds(lo, NB)]
        return remote(src, qb.at[pl.ds(0, 32)], ssem.at[2, i], rsem.at[1], k, c)

    def copy_gnc(i):
        k = other(i)
        start = pl.multiple_of(lo + k * 16, 16)
        return remote(gn.at[pl.ds(start, 16)], gc, ssem.at[3, i], rsem.at[2], k, c)

    def copy_gnr(i):
        k = other(i)
        start = pl.multiple_of(k * 64, 64)
        return remote(
            gn.at[pl.ds(start, 64), pl.ds(lo, NB)], gr, ssem.at[4, i], rsem.at[3], r, k
        )

    own_qq = pltpu.make_async_copy(piece_qq(m), qp, lsem.at[0])
    own_qqf = pltpu.make_async_copy(qp.at[pl.ds(8 * core, 8)], qb.at[pl.ds(32, 8)], lsem.at[1])
    own_jq = pltpu.make_async_copy(
        slab.at[pl.ds(32 * core, 32), pl.ds(lo, NB)], qb.at[pl.ds(0, 32)], lsem.at[2]
    )
    own_gnc = pltpu.make_async_copy(gn.at[pl.ds(lo + m * 16, 16)], gc, lsem.at[3])
    own_gnr = pltpu.make_async_copy(gn.at[pl.ds(m * 64, 64), pl.ds(lo, NB)], gr, lsem.at[4])
    trans = remote(slab, tb, ssem.at[5, 0], rsem.at[4], to_row, r)
    own_trans = pltpu.make_async_copy(slab, tb, lsem.at[7])

    def each(act, *makes):
        def body(i, carry):
            for make in makes:
                act(make(i))
            return carry

        lax.fori_loop(0, N - 1, body, 0)

    def start(copy):
        copy.start()

    def wait_send(copy):
        copy.wait_send()

    @pl.when(in_row & in_col)
    def _():
        own_qq.start()
        each(start, copy_qq)

    @pl.when(in_row)
    def _():
        own_jq.start()
        own_gnc.start()
        each(start, copy_jq, copy_gnc)

    @pl.when(in_col)
    def _():
        own_gnr.start()
        each(start, copy_gnr)

    for dim in (0, 1):
        own_j[dim].wait()
        rings[dim].begin()

    @pl.when(stays)
    def _():
        own_trans.start()

    @pl.when(jnp.logical_not(stays))
    def _():
        trans.start()

    @pl.when(in_row & in_col)
    def _():
        own_qq.wait()

    @pl.when(in_row & jnp.logical_not(in_col))
    def _():
        copy_qq(0).wait_recv()

    @pl.when(in_row)
    def _():
        own_qqf.start()
        each(start, copy_qqf)

    for dim in (0, 1):
        rings[dim].forward()

    @pl.when(in_row)
    def _():
        own_qqf.wait()
        own_jq.wait()
        own_gnc.wait()
        each(wait_send, copy_jq, copy_gnc, copy_qqf)

    @pl.when(jnp.logical_not(in_row))
    def _():
        copy_jq(0).wait_recv()
        copy_gnc(0).wait_recv()
        copy_qqf(0).wait_recv()

    @pl.when(in_col)
    def _():
        own_gnr.wait()
        each(wait_send, copy_gnr)

    @pl.when(jnp.logical_not(in_col))
    def _():
        copy_gnr(0).wait_recv()

    @pl.when(in_row & in_col)
    def _():
        each(wait_send, copy_qq)

    for dim in (0, 1):
        rings[dim].finish()
        rings[dim].drain()

    @pl.when(stays)
    def _():
        own_trans.wait()

    @pl.when(jnp.logical_not(stays))
    def _():
        trans.wait()


def spread(m, b, gn, slab):
    return pl.pallas_call(
        functools.partial(spread_kernel, m, b),
        out_shape=(
            jax.ShapeDtypeStruct((64, NB), F32),
            jax.ShapeDtypeStruct((16, 1024), F32),
            jax.ShapeDtypeStruct((40, NB), F32),
            jax.ShapeDtypeStruct((64, 1024), F32),
            jax.ShapeDtypeStruct((2, 4, 32, 1024), F32),
        ),
        in_specs=[ANY, ANY],
        out_specs=(ANY, ANY, ANY, ANY, ANY),
        scratch_shapes=[
            pltpu.VMEM((16, NB), F32),
            pltpu.SemaphoreType.DMA((6, N - 1)),
            pltpu.SemaphoreType.DMA((6,)),
            pltpu.SemaphoreType.DMA((8,)),
            pltpu.SemaphoreType.DMA((8,)),
            pltpu.SemaphoreType.DMA((8,)),
        ],
        compiler_params=pltpu.CompilerParams(
            collective_id=1 + b * N + m, has_side_effects=True
        ),
        name="spread",
    )(gn, slab)


def base(block, result):
    lane = lax.broadcasted_iota(jnp.int32, (64, 64), 1)
    sub = lax.broadcasted_iota(jnp.int32, (64, 64), 0)
    whole = jnp.concatenate([block, (lane == sub).astype(F32)], axis=1)
    rows = [whole[8 * i : 8 * i + 8] for i in range(8)]
    sub8 = lax.broadcasted_iota(jnp.int32, (8, 128), 0)

    def lanes(tile, at):
        return jnp.broadcast_to(tile[:, at : at + 1], (8, 128))

    def subs(tile, at):
        return jnp.broadcast_to(tile[at : at + 1, :], (8, 128))

    for j in range(8):
        tile = rows[j]
        cols = [lanes(tile, 8 * j + k) for k in range(8)]
        full, upper, recips = tile, tile, jnp.zeros_like(tile)
        for k in range(8):
            here = sub8 == k
            recip = 1.0 / subs(cols[k], k)
            factor = jnp.where(here, 0.0, cols[k] * recip)
            recips = jnp.where(here, recip, recips)
            upper = jnp.where(here, full, upper)
            for n in range(k + 1, 8):
                cols[n] = cols[n] - factor * subs(cols[n], k)
            full = full - factor * subs(full, k)
        solved = full * recips
        rows[j] = upper * jnp.sqrt(recips)
        spread = [subs(solved, k) for k in range(8)]
        for i in range(j + 1, 8):
            old = rows[i]
            new = old
            for k in range(8):
                new = new - lanes(old, 8 * j + k) * spread[k]
            rows[i] = new
        if j < 7:
            yield
    out = jnp.concatenate(rows, axis=0)
    result.append(jnp.where(lane >= sub, out[:, :64], 0.0))
    result.append(out[:, 64:])
    yield

def exact(left, right, dims):
    return lax.dot_general(
        left,
        right,
        (dims, ((), ())),
        precision=lax.Precision.HIGHEST,
        preferred_element_type=F32,
    )


def factor(work):
    for s in range(4):
        rows = pl.ds(64 * s, 64)
        result = []
        yield from base(work[rows, pl.ds(64 * s, 64)], result)
        upper, inverse = result
        solved = exact(inverse, work[rows, :], ((1,), (0,)))
        work[rows, :] = solved
        work[rows, pl.ds(64 * s, 64)] = upper
        if s < 3:
            rest = pl.ds(64 * (s + 1), 64 * (3 - s))
            work[rest, :] = work[rest, :] - exact(solved[:, 64 * (s + 1) : 256], solved, ((0,), (0,)))
        yield


def gather_kernel(
    ja, gr, gc, qb, tb, rg, jc, grg, gcg, jq, lower, inverse, qg, work, ssem, rsem, lsem
):
    place = Place()
    r, c, core = place.r, place.c, place.core
    turn = 8 - c // 2
    sibling = r + 1 - 2 * core
    for dim in (0, 1):
        for step in (1, -1):
            signal(r, place.col(dim, step))
    signal(place.row(1), c)
    signal(place.row(-1), c)
    signal(sibling, c)
    own_q = pltpu.make_async_copy(qb, qg.at[core, c], lsem.at[0])
    own_j = []
    for dim, at in ((0, place.x), (1, place.y)):
        for i, item in enumerate((0, -1, 1, 2)):
            src = ja.at[dim, lax.rem(at + item + 4, 4)]
            dst = rg.at[place.col2(dim, item, 0), pl.ds(32 * dim, 32)]
            own_j.append(pltpu.make_async_copy(src, dst, lsem.at[5 + 4 * dim + i]))
    own_t = pltpu.make_async_copy(
        tb, jc.at[2 * lax.rem(place.z - turn + 8, 8) + core], lsem.at[2]
    )
    own_r = pltpu.make_async_copy(gr, grg.at[c], lsem.at[3])
    own_c = pltpu.make_async_copy(gc, gcg.at[r], lsem.at[4])
    own_q.start()
    own_t.start()
    for copy in own_j:
        copy.start()
    own_c.start()
    own_r.start()
    q = Plane(place, qg.at[core], 40, ssem, rsem, 0)
    j = Plane(place, rg, 64, ssem, rsem, 40)
    g = Plane(place, grg, 64, ssem, rsem, 80)
    line = Line(place, gcg, 0, (0, 16), ssem, rsem, 120)
    t0 = Line(place, jc, turn, (0, 32), ssem, rsem, 137)
    t1 = Line(place, jc, turn, (32, 32), ssem, rsem, 154)
    swap = remote(qg.at[core], qg.at[core], ssem.at[171], rsem.at[171], sibling, c)
    swapped = remote(qg.at[1 - core], qg.at[1 - core], ssem.at[171], rsem.at[171], sibling, c)
    sub = lax.broadcasted_iota(jnp.int32, (NB, NB), 0)
    lane = lax.broadcasted_iota(jnp.int32, (NB, NB), 1)
    work[:, pl.ds(NB, NB)] = (sub == lane).astype(F32)
    pl.semaphore_wait(pltpu.get_barrier_semaphore(), 7)
    own_q.wait()
    q.begin()
    q.begin2()
    own_t.wait()
    t0.begin()
    for copy in own_j:
        copy.wait()

    def begin(item):
        for dim in (0, 1):
            j.second[dim][item].begin()

    def forward(item):
        for dim in (0, 1):
            j.second[dim][item].forward()

    begin(0)
    q.forward1()
    t1.begin()
    begin(1)
    q.forward2()
    begin(2)
    q.forward3()
    t0.step(1)
    forward(0)
    q.forward4()
    begin(3)
    t1.step(1)
    for item in range(4):
        q.finish(item)
    swap.start()
    forward(1)
    t0.step(2)
    own_r.wait()
    g.begin()
    g.begin2()
    own_c.wait()
    line.begin()
    swapped.wait_recv()
    jq[...] = jnp.stack([qg[0, :, pl.ds(0, 32), :], qg[1, :, pl.ds(0, 32), :]], axis=1)
    pivot = jnp.stack([qg[0, :, pl.ds(32, 8), :], qg[1, :, pl.ds(32, 8), :]], axis=1)
    whole = jq[...].reshape(1024, NB)
    work[:, pl.ds(0, NB)] = pivot.reshape(NB, NB) + exact(whole, whole, ((0,), (0,)))
    chain = factor(work)

    def advance(steps):
        for _ in range(steps):
            next(chain, None)

    forward(2)
    t1.step(2)
    line.step(1)
    advance(3)
    g.forward1()
    forward(3)
    advance(3)
    t0.step(3)
    line.step(2)
    advance(3)
    g.forward2()
    t1.step(3)
    advance(3)
    line.step(3)
    g.forward3()
    advance(3)
    t0.last()
    g.forward4()
    advance(3)
    t1.last()
    line.last()
    advance(40)
    lower[...] = jnp.where(sub >= lane, work[:, pl.ds(0, NB)].T, 0.0)
    inverse[...] = jnp.where(sub >= lane, work[:, pl.ds(NB, NB)], 0.0)
    t0.finish()
    t1.finish()
    line.finish()
    for item in range(4):
        j.finish(item)
        g.finish(item)
    for part in (q, g, line, t0, t1):
        part.drain()
    for dim in (0, 1):
        for ring in j.second[dim]:
            ring.drain()
    swap.wait_send()


def gather(ja, gr, gc, qb, tb):
    vmem = pl.BlockSpec(memory_space=pltpu.VMEM)
    dma = pltpu.SemaphoreType.DMA
    return pl.pallas_call(
        gather_kernel,
        out_shape=tuple(
            jax.ShapeDtypeStruct(shape, F32)
            for shape in (
                (N, 64, 1024),
                (N, 64, 1024),
                (N, 64, NB),
                (N, 16, 1024),
                (N, 2, 32, NB),
                (NB, NB),
                (NB, NB),
            )
        ),
        in_specs=[ANY] * 5,
        out_specs=(ANY, ANY, ANY, ANY, vmem, vmem, vmem),
        scratch_shapes=[
            pltpu.VMEM((2, N, 40, NB), F32),
            pltpu.VMEM((NB, 2 * NB), F32),
            dma((172,)),
            dma((172,)),
            dma((13,)),
        ],
        compiler_params=pltpu.CompilerParams(
            collective_id=0, has_side_effects=True, vmem_limit_bytes=32 * 1024 * 1024
        ),
        name="gather",
    )(ja, gr, gc, qb, tb)


def split(value):
    high = value.astype(jnp.bfloat16)
    return high, (value - high.astype(F32)).astype(jnp.bfloat16)


def side(value, axis):
    high, low = split(value)
    return jnp.concatenate([high, low, high] if axis else [low, high, high], axis=axis)


def update_kernel(
    where, gn, jr, jc, gnr, gnc, jq, lower, inverse, out, right, jq_right, inv_right
):
    which, r, c = where[0], where[1], where[2]
    step = pl.program_id(0)

    @pl.when(step == 0)
    def _():
        high, low = split(jc[...])
        right[0:1024] = low
        right[1024:2048] = high
        right[2048:3072] = high
        jq_right[...] = side(jq[...], 0)
        inv_right[...] = side(inverse[...].T, 0)
        part = gnc[...] + jnp.dot(
            side(jq[...].T, 1), right[0:3072], preferred_element_type=F32
        )
        solved = jnp.dot(side(inverse[...], 1), side(part, 0), preferred_element_type=F32)
        ids = lax.broadcasted_iota(jnp.int32, (NB, 1024), 1) // NB * N + c
        right[3072:3840] = side(jnp.where(ids > which, -solved, 0.0), 0)

    here = pl.multiple_of(step * ROWS, ROWS)
    rows = side(jr[:, pl.ds(here, ROWS)].T, 1)
    part = gnr[pl.ds(here, ROWS)] + jnp.dot(rows, jq_right[...], preferred_element_type=F32)
    solved = jnp.dot(side(part, 1), inv_right[...], preferred_element_type=F32)
    row = (step * ROWS + lax.broadcasted_iota(jnp.int32, (ROWS, NB), 0)) // NB * N + r
    below = side(jnp.where(row > which, solved, 0.0), 1)
    factor_rows = jnp.concatenate([lower[...]] * (ROWS // NB), axis=0)
    column = jnp.where(row == which, factor_rows, jnp.where(row > which, solved, part))
    for block in range(4):
        cols = slice(NB * block, NB * block + NB)
        whole = gn[:, cols] + jnp.dot(rows, right[0:3072, cols], preferred_element_type=F32)
        whole = whole + jnp.dot(below, right[3072:3840, cols], preferred_element_type=F32)
        out[:, cols] = jnp.where(block * N + c == which, column, whole)


def update(where, gn, jr, jc, gnr, gnc, jq, lower, inverse):
    bf16 = jnp.bfloat16
    return pl.pallas_call(
        update_kernel,
        out_shape=jax.ShapeDtypeStruct((1024, 1024), F32),
        grid_spec=pltpu.PrefetchScalarGridSpec(
            num_scalar_prefetch=1,
            grid=(1024 // ROWS,),
            in_specs=[pl.BlockSpec((ROWS, 1024), lambda i, where: (i, 0))]
            + [pl.BlockSpec(memory_space=pltpu.VMEM)] * 7,
            out_specs=pl.BlockSpec((ROWS, 1024), lambda i, where: (i, 0)),
            scratch_shapes=[
                pltpu.VMEM((3840, 1024), bf16),
                pltpu.VMEM((3072, NB), bf16),
                pltpu.VMEM((3 * NB, NB), bf16),
            ],
        ),
        compiler_params=pltpu.CompilerParams(
            dimension_semantics=("arbitrary",), vmem_limit_bytes=36 * 1024 * 1024
        ),
        name="update",
    )(where, gn, jr, jc, gnr, gnc, jq, lower, inverse)


def on_device(gn, slab, panel_index):
    r = lax.axis_index("row").astype(jnp.int32)
    c = lax.axis_index("col").astype(jnp.int32)
    which = panel_index[0]
    variants = [functools.partial(spread, k % N, k // N) for k in range(2 * N)]
    gr, gc, qb, tb, ja = lax.switch(which, variants, gn, slab)
    rg, jc, grg, gcg, jq, lower, inverse = gather(ja, gr, gc, qb, tb)
    return update(
        jnp.stack([which, r, c]),
        gn,
        rg.reshape(1024, 1024),
        jc.reshape(1024, 1024),
        grg.reshape(1024, NB),
        gcg.reshape(NB, 1024),
        jq.reshape(1024, NB),
        lower,
        inverse,
    )


def solution(mesh):
    return jax.shard_map(
        on_device,
        mesh=mesh,
        in_specs=(P("row", "col"), P("col", "row"), P()),
        out_specs=P("row", "col"),
        check_vma=False,
    )
```

```python
import functools

import jax
import jax.numpy as jnp
from jax import lax
from jax.experimental import pallas as pl
from jax.experimental.pallas import tpu as pltpu
from jax.sharding import PartitionSpec as P

NB = 256
ROWS = 512
N = 16
MESH = pl.DeviceIdType.MESH
ANY = pl.BlockSpec(memory_space=pl.ANY)
F32 = jnp.float32


def signal(row, col):
    pl.semaphore_signal(
        pltpu.get_barrier_semaphore(),
        inc=1,
        device_id={"row": row, "col": col},
        device_id_type=MESH,
    )


def remote(src, dst, send, recv, row, col):
    return pltpu.make_async_remote_copy(
        src_ref=src,
        dst_ref=dst,
        send_sem=send,
        recv_sem=recv,
        device_id={"row": row, "col": col},
        device_id_type=MESH,
    )


class Place:
    def __init__(self):
        self.r = lax.axis_index("row")
        self.c = lax.axis_index("col")
        self.z, self.core = self.r // 2, lax.rem(self.r, 2)
        self.x, self.y = self.c // 4, lax.rem(self.c, 4)

    def col(self, dim, step):
        if dim == 0:
            return lax.rem(self.x + step + 4, 4) * 4 + self.y
        return self.x * 4 + lax.rem(self.y + step + 4, 4)

    def col2(self, dim, first, second):
        dx, dy = (first, second) if dim == 0 else (second, first)
        return lax.rem(self.x + dx + 4, 4) * 4 + lax.rem(self.y + dy + 4, 4)

    def row(self, step):
        return lax.rem(self.z + step + 8, 8) * 2 + self.core


class Ring:
    def __init__(self, place, buf, dim, item, slot, rows, sems):
        start, height = rows
        ssem, rsem, base = sems
        plus, minus = place.col(dim, 1), place.col(dim, -1)
        half = (height // 2 + 7) // 8 * 8
        rest = height - half

        def part(at, first, size):
            return buf.at[at, pl.ds(first, size)]

        def make(n, at, first, size, target):
            ref = part(at, first, size)
            return remote(ref, ref, ssem.at[base + n], rsem.at[base + n], place.r, target)

        self.sp = make(0, slot(0), start, height, plus)
        self.sm = make(1, slot(0), start, height, minus)
        self.fp = make(2, slot(-1), start, half, plus)
        self.fm = make(3, slot(1), start + half, rest, minus)
        self.rp = make(0, slot(-1), start, height, plus)
        self.rm = make(1, slot(1), start, height, minus)
        self.rfp = make(2, slot(2), start, half, plus)
        self.rfm = make(3, slot(2), start + half, rest, minus)

    def begin(self):
        self.sp.start()
        self.sm.start()

    def forward(self):
        self.rp.wait_recv()
        self.fp.start()
        self.rm.wait_recv()
        self.fm.start()

    def finish(self):
        self.rfp.wait_recv()
        self.rfm.wait_recv()

    def drain(self):
        for copy in (self.sp, self.sm, self.fp, self.fm):
            copy.wait_send()


class Plane:
    def __init__(self, place, buf, height, ssem, rsem, base):
        half = (height // 2 + 7) // 8 * 8
        self.first, self.second = [], []
        n = base
        for dim in (0, 1):
            rows = (dim * half, half if dim == 0 else height - half)
            self.first.append(
                Ring(
                    place, buf, dim, 0,
                    functools.partial(place.col2, dim, second=0),
                    rows, (ssem, rsem, n),
                )
            )
            n += 4
            seconds = []
            for item in (0, -1, 1, 2):
                def slot(step, dim=dim, item=item):
                    return place.col2(dim, item, step)

                seconds.append(Ring(place, buf, 1 - dim, item, slot, rows, (ssem, rsem, n)))
                n += 4
            self.second.append(seconds)

    def begin(self):
        for dim in (0, 1):
            self.first[dim].begin()

    def begin2(self):
        for dim in (0, 1):
            self.second[dim][0].begin()

    def forward1(self):
        for dim in (0, 1):
            self.first[dim].forward()
        for dim in (0, 1):
            self.second[dim][1].begin()
            self.second[dim][2].begin()

    def forward2(self):
        for dim in (0, 1):
            self.second[dim][0].forward()
        for dim in (0, 1):
            self.first[dim].finish()
            self.second[dim][3].begin()

    def forward3(self):
        for item in (1, 2):
            for dim in (0, 1):
                self.second[dim][item].forward()

    def forward4(self):
        for dim in (0, 1):
            self.second[dim][3].forward()

    def finish(self, item):
        for dim in (0, 1):
            self.second[dim][item].finish()

    def drain(self):
        for dim in (0, 1):
            self.first[dim].drain()
            for ring in self.second[dim]:
                ring.drain()


class Line:
    def __init__(self, place, buf, turn, rows, ssem, rsem, base):
        start, height = rows
        half = height // 2
        plus, minus = place.row(1), place.row(-1)
        sibling = place.r + 1 - 2 * place.core

        def slot(step):
            return 2 * lax.rem(place.z - turn + step + 32, 8) + place.core

        def make(n, at, first, size, target):
            ref = buf.at[at, pl.ds(start + first, size)]
            return remote(ref, ref, ssem.at[base + n], rsem.at[base + n], target, place.c)

        self.send, self.recv = [], []
        for s in range(3):
            self.send.append(
                (make(2 * s, slot(-s), 0, height, plus), make(2 * s + 1, slot(s), 0, height, minus))
            )
            self.recv.append(
                (
                    make(2 * s, slot(-s - 1), 0, height, plus),
                    make(2 * s + 1, slot(s + 1), 0, height, minus),
                )
            )
        self.send.append((make(6, slot(-3), 0, half, plus), make(7, slot(3), half, half, minus)))
        self.recv.append((make(6, slot(4), 0, half, plus), make(7, slot(4), half, half, minus)))
        self.over, self.back = [], []
        other = 1 - 2 * place.core
        for i, step in enumerate((0, -1, 1, -2, 2, -3, 3)):
            self.over.append(make(8 + i, slot(step), 0, height, sibling))
            self.back.append(make(8 + i, slot(step) + other, 0, height, sibling))
        for i in (0, 1):
            self.over.append(make(15 + i, slot(4), half * i, half, sibling))
            self.back.append(make(15 + i, slot(4) + other, half * i, half, sibling))

    def begin(self):
        for copy in self.send[0]:
            copy.start()
        self.over[0].start()

    def step(self, s):
        for way in (0, 1):
            self.recv[s - 1][way].wait_recv()
            self.send[s][way].start()
            self.over[2 * s - 1 + way].start()

    def last(self):
        for way in (0, 1):
            self.recv[3][way].wait_recv()
            self.over[7 + way].start()

    def finish(self):
        for copy in self.back:
            copy.wait_recv()

    def drain(self):
        for pair in self.send:
            for copy in pair:
                copy.wait_send()
        for copy in self.over:
            copy.wait_send()


def spread_kernel(m, b, gn, slab, gr, gc, qb, tb, ja, qp, ssem, rsem, lsem, psend, precv):
    r = lax.axis_index("row")
    c = lax.axis_index("col")
    lo = b * NB
    core = m % 2
    in_row = r == m
    in_col = c == m
    to_row = 2 * lax.rem(c // 2 - r // 2 + 8, 8) + lax.rem(c, 2)
    from_col = 2 * lax.rem(r // 2 + c // 2, 8) + lax.rem(r, 2)
    stays = (to_row == r) & (c == r)
    place = Place()
    rings, own_j = [], []
    for dim, at in ((0, place.x), (1, place.y)):
        def slot(step, at=at):
            return lax.rem(at + step + 4, 4)

        rows = pl.ds(32 * dim, 32)
        own_j.append(pltpu.make_async_copy(slab.at[rows], ja.at[dim, at], lsem.at[5 + dim]))
        own_j[dim].start()
        rings.append(Ring(place, ja.at[dim], dim, 0, slot, (0, 32), (psend, precv, 4 * dim)))
        for step in (1, -1):
            signal(r, place.col(dim, step))

    @pl.when(jnp.logical_not(stays))
    def _():
        signal(c, from_col)

    @pl.when(jnp.logical_not(in_col))
    def _():
        signal(r, m)

    @pl.when(jnp.logical_not(in_row))
    def _():
        signal(m, c)

    count = (in_row.astype(jnp.int32) + in_col.astype(jnp.int32)) * (N - 1) + 4
    count = count + jnp.logical_not(stays).astype(jnp.int32)
    pl.semaphore_wait(pltpu.get_barrier_semaphore(), count)

    def other(i):
        return lax.rem(i + (m + 1), N)

    def piece_qq(k):
        start = pl.multiple_of(lo + k * 16, 16)
        return gn.at[pl.ds(start, 16), pl.ds(lo, NB)]

    def half(k, size):
        return pl.ds(pl.multiple_of(lax.rem(k, 2) * size, size), size)

    def copy_qq(i):
        k = other(i)
        return remote(piece_qq(k), qp, ssem.at[0, i], rsem.at[0], m, k)

    def copy_qqf(i):
        k = other(i)
        return remote(qp.at[half(k, 8)], qb.at[pl.ds(32, 8)], ssem.at[1, i], rsem.at[5], k, c)

    def copy_jq(i):
        k = other(i)
        src = slab.at[half(k, 32), pl.ds(lo, NB)]
        return remote(src, qb.at[pl.ds(0, 32)], ssem.at[2, i], rsem.at[1], k, c)

    def copy_gnc(i):
        k = other(i)
        start = pl.multiple_of(lo + k * 16, 16)
        return remote(gn.at[pl.ds(start, 16)], gc, ssem.at[3, i], rsem.at[2], k, c)

    def copy_gnr(i):
        k = other(i)
        start = pl.multiple_of(k * 64, 64)
        return remote(
            gn.at[pl.ds(start, 64), pl.ds(lo, NB)], gr, ssem.at[4, i], rsem.at[3], r, k
        )

    own_qq = pltpu.make_async_copy(piece_qq(m), qp, lsem.at[0])
    own_qqf = pltpu.make_async_copy(qp.at[pl.ds(8 * core, 8)], qb.at[pl.ds(32, 8)], lsem.at[1])
    own_jq = pltpu.make_async_copy(
        slab.at[pl.ds(32 * core, 32), pl.ds(lo, NB)], qb.at[pl.ds(0, 32)], lsem.at[2]
    )
    own_gnc = pltpu.make_async_copy(gn.at[pl.ds(lo + m * 16, 16)], gc, lsem.at[3])
    own_gnr = pltpu.make_async_copy(gn.at[pl.ds(m * 64, 64), pl.ds(lo, NB)], gr, lsem.at[4])
    trans = remote(slab, tb, ssem.at[5, 0], rsem.at[4], to_row, r)
    own_trans = pltpu.make_async_copy(slab, tb, lsem.at[7])

    def each(act, *makes):
        def body(i, carry):
            for make in makes:
                act(make(i))
            return carry

        lax.fori_loop(0, N - 1, body, 0)

    def start(copy):
        copy.start()

    def wait_send(copy):
        copy.wait_send()

    @pl.when(in_row & in_col)
    def _():
        own_qq.start()
        each(start, copy_qq)

    @pl.when(in_row)
    def _():
        own_jq.start()
        own_gnc.start()
        each(start, copy_jq, copy_gnc)

    @pl.when(in_col)
    def _():
        own_gnr.start()
        each(start, copy_gnr)

    for dim in (0, 1):
        own_j[dim].wait()
        rings[dim].begin()

    @pl.when(stays)
    def _():
        own_trans.start()

    @pl.when(jnp.logical_not(stays))
    def _():
        trans.start()

    @pl.when(in_row & in_col)
    def _():
        own_qq.wait()

    @pl.when(in_row & jnp.logical_not(in_col))
    def _():
        copy_qq(0).wait_recv()

    @pl.when(in_row)
    def _():
        own_qqf.start()
        each(start, copy_qqf)

    for dim in (0, 1):
        rings[dim].forward()

    @pl.when(in_row)
    def _():
        own_qqf.wait()
        own_jq.wait()
        own_gnc.wait()
        each(wait_send, copy_jq, copy_gnc, copy_qqf)

    @pl.when(jnp.logical_not(in_row))
    def _():
        copy_jq(0).wait_recv()
        copy_gnc(0).wait_recv()
        copy_qqf(0).wait_recv()

    @pl.when(in_col)
    def _():
        own_gnr.wait()
        each(wait_send, copy_gnr)

    @pl.when(jnp.logical_not(in_col))
    def _():
        copy_gnr(0).wait_recv()

    @pl.when(in_row & in_col)
    def _():
        each(wait_send, copy_qq)

    for dim in (0, 1):
        rings[dim].finish()
        rings[dim].drain()

    @pl.when(stays)
    def _():
        own_trans.wait()

    @pl.when(jnp.logical_not(stays))
    def _():
        trans.wait()


def spread(m, b, gn, slab):
    return pl.pallas_call(
        functools.partial(spread_kernel, m, b),
        out_shape=(
            jax.ShapeDtypeStruct((64, NB), F32),
            jax.ShapeDtypeStruct((16, 1024), F32),
            jax.ShapeDtypeStruct((40, NB), F32),
            jax.ShapeDtypeStruct((64, 1024), F32),
            jax.ShapeDtypeStruct((2, 4, 32, 1024), F32),
        ),
        in_specs=[ANY, ANY],
        out_specs=(ANY, ANY, ANY, ANY, ANY),
        scratch_shapes=[
            pltpu.VMEM((16, NB), F32),
            pltpu.SemaphoreType.DMA((6, N - 1)),
            pltpu.SemaphoreType.DMA((6,)),
            pltpu.SemaphoreType.DMA((8,)),
            pltpu.SemaphoreType.DMA((8,)),
            pltpu.SemaphoreType.DMA((8,)),
        ],
        compiler_params=pltpu.CompilerParams(
            collective_id=1 + b * N + m, has_side_effects=True
        ),
        name="spread",
    )(gn, slab)


def base(block, result):
    lane = lax.broadcasted_iota(jnp.int32, (64, 64), 1)
    sub = lax.broadcasted_iota(jnp.int32, (64, 64), 0)
    whole = jnp.concatenate([block, (lane == sub).astype(F32)], axis=1)
    rows = [whole[8 * i : 8 * i + 8] for i in range(8)]
    sub8 = lax.broadcasted_iota(jnp.int32, (8, 128), 0)

    def lanes(tile, at):
        return jnp.broadcast_to(tile[:, at : at + 1], (8, 128))

    def subs(tile, at):
        return jnp.broadcast_to(tile[at : at + 1, :], (8, 128))

    for j in range(8):
        tile = rows[j]
        cols = [lanes(tile, 8 * j + k) for k in range(8)]
        full, upper, recips = tile, tile, jnp.zeros_like(tile)
        for k in range(8):
            here = sub8 == k
            recip = 1.0 / subs(cols[k], k)
            factor = jnp.where(here, 0.0, cols[k] * recip)
            recips = jnp.where(here, recip, recips)
            upper = jnp.where(here, full, upper)
            for n in range(k + 1, 8):
                cols[n] = cols[n] - factor * subs(cols[n], k)
            full = full - factor * subs(full, k)
        solved = full * recips
        rows[j] = upper * jnp.sqrt(recips)
        spread = [subs(solved, k) for k in range(8)]
        for i in range(j + 1, 8):
            old = rows[i]
            new = old
            for k in range(8):
                new = new - lanes(old, 8 * j + k) * spread[k]
            rows[i] = new
        if j < 7:
            yield
    out = jnp.concatenate(rows, axis=0)
    result.append(jnp.where(lane >= sub, out[:, :64], 0.0))
    result.append(out[:, 64:])
    yield

def exact(left, right, dims):
    return lax.dot_general(
        left,
        right,
        (dims, ((), ())),
        precision=lax.Precision.HIGHEST,
        preferred_element_type=F32,
    )


def factor(work):
    for s in range(4):
        rows = pl.ds(64 * s, 64)
        result = []
        yield from base(work[rows, pl.ds(64 * s, 64)], result)
        upper, inverse = result
        solved = exact(inverse, work[rows, :], ((1,), (0,)))
        work[rows, :] = solved
        work[rows, pl.ds(64 * s, 64)] = upper
        if s < 3:
            rest = pl.ds(64 * (s + 1), 64 * (3 - s))
            work[rest, :] = work[rest, :] - exact(solved[:, 64 * (s + 1) : 256], solved, ((0,), (0,)))
        yield


def gather_kernel(
    ja, gr, gc, qb, tb, rg, jc, grg, gcg, jq, lower, inverse, qg, work, ssem, rsem, lsem
):
    place = Place()
    r, c, core = place.r, place.c, place.core
    turn = 8 - c // 2
    sibling = r + 1 - 2 * core
    for dim in (0, 1):
        for step in (1, -1):
            signal(r, place.col(dim, step))
    signal(place.row(1), c)
    signal(place.row(-1), c)
    signal(sibling, c)
    own_q = pltpu.make_async_copy(qb, qg.at[core, c], lsem.at[0])
    own_j = []
    for dim, at in ((0, place.x), (1, place.y)):
        for i, item in enumerate((0, -1, 1, 2)):
            src = ja.at[dim, lax.rem(at + item + 4, 4)]
            dst = rg.at[place.col2(dim, item, 0), pl.ds(32 * dim, 32)]
            own_j.append(pltpu.make_async_copy(src, dst, lsem.at[5 + 4 * dim + i]))
    own_t = pltpu.make_async_copy(
        tb, jc.at[2 * lax.rem(place.z - turn + 8, 8) + core], lsem.at[2]
    )
    own_r = pltpu.make_async_copy(gr, grg.at[c], lsem.at[3])
    own_c = pltpu.make_async_copy(gc, gcg.at[r], lsem.at[4])
    own_q.start()
    own_t.start()
    for copy in own_j:
        copy.start()
    own_c.start()
    own_r.start()
    q = Plane(place, qg.at[core], 40, ssem, rsem, 0)
    j = Plane(place, rg, 64, ssem, rsem, 40)
    g = Plane(place, grg, 64, ssem, rsem, 80)
    line = Line(place, gcg, 0, (0, 16), ssem, rsem, 120)
    t0 = Line(place, jc, turn, (0, 32), ssem, rsem, 137)
    t1 = Line(place, jc, turn, (32, 32), ssem, rsem, 154)
    swap = remote(qg.at[core], qg.at[core], ssem.at[171], rsem.at[171], sibling, c)
    swapped = remote(qg.at[1 - core], qg.at[1 - core], ssem.at[171], rsem.at[171], sibling, c)
    sub = lax.broadcasted_iota(jnp.int32, (NB, NB), 0)
    lane = lax.broadcasted_iota(jnp.int32, (NB, NB), 1)
    work[:, pl.ds(NB, NB)] = (sub == lane).astype(F32)
    pl.semaphore_wait(pltpu.get_barrier_semaphore(), 7)
    own_q.wait()
    q.begin()
    q.begin2()
    own_t.wait()
    t0.begin()
    for copy in own_j:
        copy.wait()

    def begin(item):
        for dim in (0, 1):
            j.second[dim][item].begin()

    def forward(item):
        for dim in (0, 1):
            j.second[dim][item].forward()

    begin(0)
    q.forward1()
    t1.begin()
    begin(1)
    own_c.wait()
    line.begin()
    q.forward2()
    begin(2)
    q.forward3()
    t0.step(1)
    own_r.wait()
    g.begin()
    forward(0)
    q.forward4()
    begin(3)
    t1.step(1)
    line.step(1)
    for item in range(4):
        q.finish(item)
    swap.start()
    g.begin2()
    forward(1)
    t0.step(2)
    swapped.wait_recv()
    jq[...] = jnp.stack([qg[0, :, pl.ds(0, 32), :], qg[1, :, pl.ds(0, 32), :]], axis=1)
    pivot = jnp.stack([qg[0, :, pl.ds(32, 8), :], qg[1, :, pl.ds(32, 8), :]], axis=1)
    whole = jq[...].reshape(1024, NB)
    work[:, pl.ds(0, NB)] = pivot.reshape(NB, NB) + exact(whole, whole, ((0,), (0,)))
    chain = factor(work)

    def advance(steps):
        for _ in range(steps):
            next(chain, None)

    forward(2)
    t1.step(2)
    line.step(2)
    advance(3)
    g.forward1()
    forward(3)
    advance(3)
    t0.step(3)
    line.step(3)
    g.forward2()
    advance(3)
    t1.step(3)
    line.last()
    g.forward3()
    advance(3)
    t0.last()
    g.forward4()
    advance(3)
    t1.last()
    advance(40)
    lower[...] = jnp.where(sub >= lane, work[:, pl.ds(0, NB)].T, 0.0)
    inverse[...] = jnp.where(sub >= lane, work[:, pl.ds(NB, NB)], 0.0)
    t0.finish()
    t1.finish()
    line.finish()
    for item in range(4):
        j.finish(item)
        g.finish(item)
    for part in (q, g, line, t0, t1):
        part.drain()
    for dim in (0, 1):
        for ring in j.second[dim]:
            ring.drain()
    swap.wait_send()


def gather(ja, gr, gc, qb, tb):
    vmem = pl.BlockSpec(memory_space=pltpu.VMEM)
    dma = pltpu.SemaphoreType.DMA
    return pl.pallas_call(
        gather_kernel,
        out_shape=tuple(
            jax.ShapeDtypeStruct(shape, F32)
            for shape in (
                (N, 64, 1024),
                (N, 64, 1024),
                (N, 64, NB),
                (N, 16, 1024),
                (N, 2, 32, NB),
                (NB, NB),
                (NB, NB),
            )
        ),
        in_specs=[ANY] * 5,
        out_specs=(ANY, ANY, ANY, ANY, vmem, vmem, vmem),
        scratch_shapes=[
            pltpu.VMEM((2, N, 40, NB), F32),
            pltpu.VMEM((NB, 2 * NB), F32),
            dma((172,)),
            dma((172,)),
            dma((13,)),
        ],
        compiler_params=pltpu.CompilerParams(
            collective_id=0, has_side_effects=True, vmem_limit_bytes=32 * 1024 * 1024
        ),
        name="gather",
    )(ja, gr, gc, qb, tb)


def split(value):
    high = value.astype(jnp.bfloat16)
    return high, (value - high.astype(F32)).astype(jnp.bfloat16)


def side(value, axis):
    high, low = split(value)
    return jnp.concatenate([high, low, high] if axis else [low, high, high], axis=axis)


def update_kernel(
    where, gn, jr, jc, gnr, gnc, jq, lower, inverse, out, right, jq_right, inv_right
):
    which, r, c = where[0], where[1], where[2]
    step = pl.program_id(0)

    @pl.when(step == 0)
    def _():
        high, low = split(jc[...])
        right[0:1024] = low
        right[1024:2048] = high
        right[2048:3072] = high
        jq_right[...] = side(jq[...], 0)
        inv_right[...] = side(inverse[...].T, 0)
        part = gnc[...] + jnp.dot(
            side(jq[...].T, 1), right[0:3072], preferred_element_type=F32
        )
        solved = jnp.dot(side(inverse[...], 1), side(part, 0), preferred_element_type=F32)
        ids = lax.broadcasted_iota(jnp.int32, (NB, 1024), 1) // NB * N + c
        right[3072:3840] = side(jnp.where(ids > which, -solved, 0.0), 0)

    here = pl.multiple_of(step * ROWS, ROWS)
    rows = side(jr[:, pl.ds(here, ROWS)].T, 1)
    part = gnr[pl.ds(here, ROWS)] + jnp.dot(rows, jq_right[...], preferred_element_type=F32)
    solved = jnp.dot(side(part, 1), inv_right[...], preferred_element_type=F32)
    row = (step * ROWS + lax.broadcasted_iota(jnp.int32, (ROWS, NB), 0)) // NB * N + r
    below = side(jnp.where(row > which, solved, 0.0), 1)
    factor_rows = jnp.concatenate([lower[...]] * (ROWS // NB), axis=0)
    column = jnp.where(row == which, factor_rows, jnp.where(row > which, solved, part))
    for block in range(4):
        cols = slice(NB * block, NB * block + NB)
        whole = gn[:, cols] + jnp.dot(rows, right[0:3072, cols], preferred_element_type=F32)
        whole = whole + jnp.dot(below, right[3072:3840, cols], preferred_element_type=F32)
        out[:, cols] = jnp.where(block * N + c == which, column, whole)


def update(where, gn, jr, jc, gnr, gnc, jq, lower, inverse):
    bf16 = jnp.bfloat16
    return pl.pallas_call(
        update_kernel,
        out_shape=jax.ShapeDtypeStruct((1024, 1024), F32),
        grid_spec=pltpu.PrefetchScalarGridSpec(
            num_scalar_prefetch=1,
            grid=(1024 // ROWS,),
            in_specs=[pl.BlockSpec((ROWS, 1024), lambda i, where: (i, 0))]
            + [pl.BlockSpec(memory_space=pltpu.VMEM)] * 7,
            out_specs=pl.BlockSpec((ROWS, 1024), lambda i, where: (i, 0)),
            scratch_shapes=[
                pltpu.VMEM((3840, 1024), bf16),
                pltpu.VMEM((3072, NB), bf16),
                pltpu.VMEM((3 * NB, NB), bf16),
            ],
        ),
        compiler_params=pltpu.CompilerParams(
            dimension_semantics=("arbitrary",), vmem_limit_bytes=36 * 1024 * 1024
        ),
        name="update",
    )(where, gn, jr, jc, gnr, gnc, jq, lower, inverse)


def on_device(gn, slab, panel_index):
    r = lax.axis_index("row").astype(jnp.int32)
    c = lax.axis_index("col").astype(jnp.int32)
    which = panel_index[0]
    variants = [functools.partial(spread, k % N, k // N) for k in range(2 * N)]
    gr, gc, qb, tb, ja = lax.switch(which, variants, gn, slab)
    rg, jc, grg, gcg, jq, lower, inverse = gather(ja, gr, gc, qb, tb)
    return update(
        jnp.stack([which, r, c]),
        gn,
        rg.reshape(1024, 1024),
        jc.reshape(1024, 1024),
        grg.reshape(1024, NB),
        gcg.reshape(NB, 1024),
        jq.reshape(1024, NB),
        lower,
        inverse,
    )


def solution(mesh):
    return jax.shard_map(
        on_device,
        mesh=mesh,
        in_specs=(P("row", "col"), P("col", "row"), P()),
        out_specs=P("row", "col"),
        check_vma=False,
    )
```
